512 devices in a mesh: kv: 8 (over y, core), ctx: 64 (over x, z).
Axes of the slice: x: 4, y: 4, z: 16, core: 2. Of those that a mesh axis runs over, the one named last changes fastest.
Arguments:
- queries: bfloat16 [128, 16384], P('ctx', 'kv'), may hold values from -30 to 30
- cache_keys: bfloat16 [131072, 1024], P('ctx', 'kv'), may hold values from -12 to 12
- cache_values: bfloat16 [131072, 1024], P('ctx', 'kv'), may hold values from -6 to 6
- out_weight: bfloat16 [16384, 16384], P('kv', 'ctx'), may hold values from -0.046875 to 0.046875
- cached_length: int32 [1], replicated, may hold values from 124928 to 126975
- start: int32 [1], replicated, may hold values from 129024 to 130944
Outputs:
- projected: bfloat16 [128, 16384], P('kv', 'ctx')
The draws below stay inside these ranges and needn't reach their ends.
All inputs are finite; a program needn't handle non-finite values.
Results may differ from the reference program's by a relative error of at most 0.0049.
Values may be sent and summed in bfloat16 or wider, within the bound.
No kernel may reach another device: no remote copies, remote signals or barrier semaphores. Data moves between devices by JAX's collectives and lax.ppermute only.
A program may use at most 64 MiB of HBM per device.

```python
import math
import jax
import jax.numpy as jnp
from jax import lax

HD = 128
GROUP = 16
KVH = 8
HEADS = 128
D = 16384
S_DEV = 2048
CTX = 131072
QTOK = 128


def draw_cache_keys(key, part):
    key = jax.random.fold_in(key, 3)
    drawn = jnp.clip(2.0 * jax.random.normal(key, (CTX, KVH * HD), jnp.float32), -12.0, 12.0)
    return drawn.astype(jnp.bfloat16)


def draw_queries(key, part):
    key = jax.random.fold_in(key, 5)
    drawn = jnp.clip(1.5 * jax.random.normal(key, (QTOK, HEADS * HD), jnp.float32), -9.0, 9.0)
    return drawn.astype(jnp.bfloat16)


def steps_of(stream_key, shape, cuts, low, top_value):
    def one(dim, blocks):
        steps = jax.random.uniform(jax.random.fold_in(jax.random.fold_in(stream_key, 6), dim), (blocks,), jnp.float32, low / len(cuts), top_value / len(cuts))
        return jnp.repeat(jnp.exp(steps), shape[dim] // blocks).reshape((-1,) + (1,) * (len(shape) - dim - 1))

    gain = one(*cuts[0])
    for cut in cuts[1:]:
        gain = gain * one(*cut)
    return gain


def scatter_about(rng, extent, scale, limit, cuts=(), kind=jnp.bfloat16):
    values = jax.random.normal(rng, extent, jnp.float32) * scale
    if len(cuts) > 0:
        values = steps_of(rng, extent, cuts, -0.22, 0.18) * values
    return jnp.clip(values, min=-limit, max=limit).astype(kind)


def setup_inputs(seed: int = 0) -> dict:
    key_list = jax.random.split(jax.random.key(seed), 7)
    queries = draw_queries(jax.random.fold_in(key_list[6], 71), 0)
    cache_keys = draw_cache_keys(jax.random.fold_in(key_list[6], 71), 0)
    cache_values = scatter_about(key_list[2], (CTX, KVH * HD), 1.0, 6.0, ((0, 64), (1, 8)))
    out_weight = scatter_about(key_list[3], (HEADS * HD, D), (HEADS * HD) ** -0.5, 0.046875, ((0, 8), (1, 64)))
    cached_length = jax.random.randint(key_list[4], (1,), CTX - 3 * S_DEV, CTX - 2 * S_DEV).astype(jnp.int32)
    start = jax.random.randint(key_list[5], (1,), CTX - S_DEV, CTX - QTOK + 1).astype(jnp.int32)
    return {"queries": queries, "cache_keys": cache_keys, "cache_values": cache_values, "out_weight": out_weight, "cached_length": cached_length, "start": start}


floor_score = -1e+30

def reference(queries, cache_keys, cache_values, out_weight, cached_length, start):
    block_len = min(512, S_DEV)
    block_count = CTX // block_len
    query_heads = queries.astype(jnp.float32).reshape(QTOK, KVH, GROUP, HD)
    score_scale = 1.0 / math.sqrt(HD)
    token_ids = jnp.arange(QTOK, dtype=jnp.int32)[:, None]
    cached_end = cached_length[0]
    span_start = start[0]

    def advance(state, block_id):
        run_max, run_sum, run_out = state
        key_base = block_id * block_len
        keys = lax.dynamic_slice_in_dim(cache_keys, key_base, block_len, 0).astype(jnp.float32).reshape(block_len, KVH, HD)
        values = lax.dynamic_slice_in_dim(cache_values, key_base, block_len, 0).astype(jnp.float32).reshape(block_len, KVH, HD)
        scores = jnp.einsum('tkgd,skd->tkgs', query_heads, keys) * score_scale
        key_pos = key_base + jnp.arange(block_len, dtype=jnp.int32)[None, :]
        visible = (key_pos < cached_end) | (key_pos >= span_start) & (key_pos <= span_start + token_ids)
        visible = visible[:, None, None, :]
        block_max = lax.optimization_barrier(jnp.max(jnp.where(visible, scores, floor_score), axis=-1))
        weights = jnp.where(visible, jnp.exp(scores - block_max[..., None]), 0.0)
        block_sum = lax.optimization_barrier(jnp.sum(weights, axis=-1))
        block_out = jnp.einsum('tkgs,skd->tkgd', weights.astype(jnp.bfloat16).astype(jnp.float32), values)
        new_max = jnp.maximum(run_max, block_max)
        keep_old = jnp.exp(run_max - new_max)
        keep_new = jnp.exp(block_max - new_max)
        run_sum = run_sum * keep_old + block_sum * keep_new
        run_out = run_out * keep_old[..., None] + block_out * keep_new[..., None]
        return ((new_max, run_sum, run_out), None)
    init_state = (jnp.full((QTOK, KVH, GROUP), floor_score, jnp.float32), jnp.zeros((QTOK, KVH, GROUP), jnp.float32), jnp.zeros((QTOK, KVH, GROUP, HD), jnp.float32))
    final_state, unused = lax.scan(advance, init_state, jnp.arange(block_count, dtype=jnp.int32))
    run_max, run_sum, run_out = final_state
    attention = (run_out / run_sum[..., None]).reshape(QTOK, HEADS * HD).astype(jnp.bfloat16)
    return jnp.dot(attention, out_weight, preferred_element_type=jnp.float32).astype(jnp.bfloat16)
```

```python
import math

import jax
import jax.numpy as jnp
from jax import lax
from jax.experimental import pallas as pl
from jax.experimental.pallas import tpu as pltpu
from jax.sharding import Mesh
from jax.sharding import PartitionSpec as P

HD = 128
GROUP = 16
SCALE2 = math.log2(math.e) / math.sqrt(HD)
X, ZH, ZL = 4, 4, 4
OWNERS = X * ZL
STAT = 16
ROWS = HD + STAT
KEY_BLOCK = 256
HIDDEN = -1e30
LOWEST = -1e5

bf16 = jnp.bfloat16
f32 = jnp.float32
ROW_ROW = (((1,), (1,)), ((), ()))
ROW_COL = (((1,), (0,)), ((), ()))


def in_vmem(count):
    return [pl.BlockSpec(memory_space=pltpu.VMEM)] * count


def pack(out, top, total):
    high = total.astype(bf16).astype(f32)
    blank = jnp.zeros((STAT - 3, out.shape[1]), f32)
    return jnp.concatenate([out, top, high, total - high, blank], axis=0).astype(bf16)


def attend_kernel(info_ref, q_ref, k_ref, v_ref, o_ref, vt_ref, s_ref):
    keys = k_ref.shape[0]
    blocks = keys // KEY_BLOCK
    pairs = OWNERS // 2
    key_base, cached_end, span_start = info_ref[0], info_ref[1], info_ref[2]
    vt_ref[:HD, :] = v_ref[...].astype(f32).T.astype(bf16)
    vt_ref[HD:, :] = jnp.ones((STAT, keys), bf16)

    def query_rows(pair):
        parts = []
        for owner in (2 * pair, 2 * pair + 1):
            x, zl = owner // ZL, owner % ZL
            for zh in range(ZH):
                at = ((x * ZH + zh) * ZL + zl) * 2 * GROUP
                parts.append(q_ref[at : at + 2 * GROUP, :])
        return jnp.concatenate(parts, axis=0)

    def score(pair, masked):
        rows = query_rows(pair)
        top = None
        for block in range(blocks):
            span = slice(block * KEY_BLOCK, (block + 1) * KEY_BLOCK)
            s = lax.dot_general(k_ref[span, :], rows, ROW_ROW, preferred_element_type=f32)
            if masked:
                pos = key_base + block * KEY_BLOCK + lax.broadcasted_iota(jnp.int32, s.shape, 0)
                col = lax.broadcasted_iota(jnp.int32, s.shape, 1)
                owner = 2 * pair + (col >> 7)
                token = (
                    (owner >> 2) * 32 + ((col >> 5) & 3) * 8 + (owner & 3) * 2 + ((col >> 4) & 1)
                )
                visible = (pos < cached_end) | (pos >= span_start) & (pos <= span_start + token)
                s = jnp.where(visible, s, HIDDEN)
            s_ref[pair % 2, span, :] = s
            here = jnp.max(s.reshape(KEY_BLOCK // 8, 8, s.shape[1]), axis=0)
            top = here if top is None else jnp.maximum(top, here)
        top = jnp.max(top, axis=0, keepdims=True) * SCALE2
        return jnp.maximum(top, LOWEST).astype(bf16).astype(f32)

    def weigh(pair, top):
        total = None
        for block in range(blocks):
            span = slice(block * KEY_BLOCK, (block + 1) * KEY_BLOCK)
            w = jnp.exp2(s_ref[pair % 2, span, :] * SCALE2 - top).astype(bf16)
            part = lax.dot_general(vt_ref[:, span], w, ROW_COL, preferred_element_type=f32)
            total = part if total is None else total + part
        message = pack(total[:HD], top, total[HD : HD + 1])
        o_ref[2 * pair] = message[:, :HD]
        o_ref[2 * pair + 1] = message[:, HD:]

    def run(masked):
        top = score(0, masked)
        for pair in range(pairs):
            following = score(pair + 1, masked) if pair + 1 < pairs else None
            weigh(pair, top)
            top = following

    whole = key_base + keys <= cached_end
    pl.when(whole)(lambda: run(False))
    pl.when(jnp.logical_not(whole))(lambda: run(True))


def attend(info, queries, keys, values):
    count = keys.shape[0]
    return pl.pallas_call(
        attend_kernel,
        out_shape=jax.ShapeDtypeStruct((OWNERS, ROWS, HD), bf16),
        in_specs=[pl.BlockSpec(memory_space=pltpu.SMEM)] + in_vmem(3),
        out_specs=pl.BlockSpec(memory_space=pltpu.VMEM),
        scratch_shapes=[
            pltpu.VMEM((ROWS, count), bf16),
            pltpu.VMEM((2, count, 2 * HD), f32),
        ],
        compiler_params=pltpu.CompilerParams(vmem_limit_bytes=24 * 2**20),
        cost_estimate=pl.CostEstimate(
            flops=4 * queries.shape[0] * count * HD,
            bytes_accessed=2 * 2**20,
            transcendentals=queries.shape[0] * count,
        ),
        name="attend",
    )(info, queries, keys, values)


def merged(in_ref):
    senders = in_ref.shape[0]
    stats = [in_ref[i, HD:, :].astype(f32) for i in range(senders)]
    tops = [s[0:1] for s in stats]
    top = tops[0]
    for other in tops[1:]:
        top = jnp.maximum(top, other)
    out, total = None, None
    for i in range(senders):
        keep = jnp.exp2(tops[i] - top)
        part = in_ref[i, :HD, :].astype(f32) * keep
        part_sum = (stats[i][1:2] + stats[i][2:3]) * keep
        out = part if out is None else out + part
        total = part_sum if total is None else total + part_sum
    return out, top, total


def merge_kernel(in_ref, o_ref):
    message = pack(*merged(in_ref))
    for i in range(o_ref.shape[0]):
        o_ref[i] = message


def merge(came, copies):
    return pl.pallas_call(
        merge_kernel,
        out_shape=jax.ShapeDtypeStruct((copies, ROWS, HD), bf16),
        in_specs=in_vmem(1),
        out_specs=pl.BlockSpec(memory_space=pltpu.VMEM),
        name="merge",
    )(came)


def finish_kernel(in_ref, o_ref, turned_ref):
    out, _, total = merged(in_ref)
    turned_ref[...] = (out / total).T
    tokens = o_ref.shape[1]
    heads = [turned_ref[pl.ds(h, tokens, stride=GROUP), :] for h in range(GROUP)]
    rows = jnp.concatenate(heads, axis=1).astype(bf16)
    for i in range(o_ref.shape[0]):
        o_ref[i] = rows


def finish(came, copies):
    return pl.pallas_call(
        finish_kernel,
        out_shape=jax.ShapeDtypeStruct((copies, HD // GROUP, GROUP * HD), bf16),
        in_specs=in_vmem(1),
        out_specs=pl.BlockSpec(memory_space=pltpu.VMEM),
        scratch_shapes=[pltpu.VMEM((HD, HD), f32)],
        name="finish",
    )(came)


def project_kernel(a_ref, w_ref, o_ref):
    owners, tokens, depth = a_ref.shape
    rows = a_ref[...].astype(f32).reshape(owners * tokens, depth).astype(bf16)
    out = jnp.dot(rows, w_ref[...], preferred_element_type=f32)
    for x in range(X):
        for zh in range(ZH):
            for zl in range(ZL):
                at = ((x * ZL + zl) * ZH + zh) * 2
                to = (zh % 2) * 8 + zl * 2
                o_ref[x * 2 + zh // 2, to : to + 2, :] = out[at : at + 2]


def project(rows, weight):
    return pl.pallas_call(
        project_kernel,
        out_shape=jax.ShapeDtypeStruct((8, 16, weight.shape[1]), f32),
        in_specs=in_vmem(2),
        out_specs=pl.BlockSpec(memory_space=pltpu.VMEM),
        name="project",
    )(rows, weight)


def exchange(parts, axes):
    return lax.all_to_all(parts, axes, split_axis=0, concat_axis=0, tiled=True)


def spread(part, axes, count):
    return exchange(jnp.broadcast_to(part[None], (count,) + part.shape), axes)


def per_device(queries, cache_keys, cache_values, out_weight, cached_length, start):
    key_base = lax.axis_index(("x", "zh", "zl")) * cache_keys.shape[0]
    info = jnp.stack([key_base, cached_length[0], start[0]]).astype(jnp.int32)
    rows = queries.reshape(2 * GROUP, HD)
    rows = spread(rows, ("zh", "zl"), ZH * ZL)
    rows = spread(rows, ("x",), X)
    rows = rows.reshape(X * ZH * ZL * 2 * GROUP, HD)
    parts = attend(info, rows, cache_keys, cache_values)
    came = exchange(parts, ("x", "zl"))
    came = exchange(merge(came, ZH), ("zh",))
    attention = exchange(finish(came, OWNERS), ("x", "zl"))
    partial_out = exchange(project(attention, out_weight), ("y", "c"))
    return jnp.sum(partial_out, axis=0).astype(bf16)


def solution(mesh):
    fine = Mesh(mesh.devices.reshape(4, 2, X, ZH, ZL), ("y", "c", "x", "zh", "zl"))
    ctx, kv = ("x", "zh", "zl"), ("y", "c")
    return jax.shard_map(
        per_device,
        mesh=fine,
        in_specs=(P(ctx, kv), P(ctx, kv), P(ctx, kv), P(kv, ctx), P(), P()),
        out_specs=P(kv, ctx),
        check_vma=False,
    )
```

```python
import math

import jax
import jax.numpy as jnp
from jax import lax
from jax.experimental import pallas as pl
from jax.experimental.pallas import tpu as pltpu
from jax.sharding import Mesh
from jax.sharding import PartitionSpec as P

HD = 128
GROUP = 16
SCALE2 = math.log2(math.e) / math.sqrt(HD)
XA, XB, ZH, ZL = 2, 2, 4, 4
OWNERS = XA * XB * ZL
STAT = 16
ROWS = HD + STAT
KEY_BLOCK = 256
HIDDEN = -1e30
LOWEST = -1e5
MIB = 2**20

bf16 = jnp.bfloat16
f32 = jnp.float32
ROW_ROW = (((1,), (1,)), ((), ()))
ROW_COL = (((1,), (0,)), ((), ()))

def in_vmem(count):
    return [pl.BlockSpec(memory_space=pltpu.VMEM)] * count

def pack(out, top, total):
    high = total.astype(bf16).astype(f32)
    blank = jnp.zeros((STAT - 3, out.shape[1]), f32)
    return jnp.concatenate([out, top, high, total - high, blank], axis=0).astype(bf16)

def attend_kernel(info_ref, qa_ref, qb_ref, k_ref, v_ref, kv_ref, o_ref, vt_ref, s_ref, hide_ref):
    near = k_ref.shape[0]
    keys = 2 * near
    blocks = keys // KEY_BLOCK
    x, near_base, far_base, cached_end, span_start = [info_ref[i] for i in range(5)]
    xb = x & 1
    vt_ref[:HD, :near] = v_ref[...].astype(f32).T.astype(bf16)
    vt_ref[:HD, near:] = kv_ref[:, HD:].astype(f32).T.astype(bf16)
    vt_ref[HD:, :] = jnp.ones((STAT, keys), bf16)
    chunks = [(q, zl) for q in (0, 1) for zl in range(0, ZL, 2)]

    def query_rows(chunk):
        q, zl0 = chunk
        ref = (qa_ref, qb_ref)[q]
        parts = []
        for zl in (zl0, zl0 + 1):
            for zh in range(ZH):
                at = (zh * ZL + zl) * 2 * GROUP
                parts.append(ref[at : at + 2 * GROUP, :])
        return jnp.concatenate(parts, axis=0)

    def key_rows(block):
        at = block * KEY_BLOCK
        if at < near:
            return k_ref[at : at + KEY_BLOCK, :]
        return kv_ref[at - near : at - near + KEY_BLOCK, :HD]

    def hide():
        for half, base in ((0, near_base), (1, far_base)):
            pos = base + lax.broadcasted_iota(jnp.int32, (near, HD), 0)
            token = lax.broadcasted_iota(jnp.int32, (near, HD), 1)
            visible = (pos < cached_end) | (pos >= span_start) & (pos <= span_start + token)
            hide_ref[half * near : (half + 1) * near, :] = jnp.where(visible, 0.0, HIDDEN).astype(bf16)

    def token_rows(chunk):
        q, zl0 = chunk
        row = lax.broadcasted_iota(jnp.int32, (2 * HD, HD), 0)
        col = lax.broadcasted_iota(jnp.int32, (2 * HD, HD), 1)
        owner = x if q == 0 else x ^ 1
        token = owner * 32 + ((row >> 5) & 3) * 8 + (zl0 + (row >> 7)) * 2 + ((row >> 4) & 1)
        return jnp.where(token == col, 1.0, 0.0).astype(bf16)

    def score(i, masked):
        rows = query_rows(chunks[i])
        if masked:
            rows = jnp.concatenate([rows, token_rows(chunks[i])], axis=1)
        top = None
        for block in range(blocks):
            span = slice(block * KEY_BLOCK, (block + 1) * KEY_BLOCK)
            left = key_rows(block)
            if masked:
                left = jnp.concatenate([left, hide_ref[span, :]], axis=1)
            s = lax.dot_general(left, rows, ROW_ROW, preferred_element_type=f32)
            s_ref[i % 2, span, :] = s
            here = jnp.max(s.reshape(KEY_BLOCK // 8, 8, s.shape[1]), axis=0)
            top = here if top is None else jnp.maximum(top, here)
        top = jnp.max(top, axis=0, keepdims=True) * SCALE2
        return jnp.maximum(top, LOWEST).astype(bf16).astype(f32)

    def weigh(i, top):
        total = None
        for block in range(blocks):
            span = slice(block * KEY_BLOCK, (block + 1) * KEY_BLOCK)
            w = jnp.exp2(s_ref[i % 2, span, :] * SCALE2 - top).astype(bf16)
            part = lax.dot_general(vt_ref[:, span], w, ROW_COL, preferred_element_type=f32)
            total = part if total is None else total + part
        message = pack(total[:HD], top, total[HD : HD + 1])
        q, zl = chunks[i]
        to = (xb if q == 0 else 1 - xb) * ZL + zl
        o_ref[to] = message[:, :HD]
        o_ref[to + 1] = message[:, HD:]

    def run(masked):
        if masked:
            hide()
        top = score(0, masked)
        for i in range(len(chunks)):
            following = score(i + 1, masked) if i + 1 < len(chunks) else None
            weigh(i, top)
            top = following
    whole = (near_base + near <= cached_end) & (far_base + near <= cached_end)
    pl.when(whole)(lambda: run(False))
    pl.when(jnp.logical_not(whole))(lambda: run(True))

def attend(info, qa, qb, keys, values, far):
    count = 2 * keys.shape[0]
    return pl.pallas_call(
        attend_kernel,
        out_shape=jax.ShapeDtypeStruct((XB * ZL, ROWS, HD), bf16),
        in_specs=[pl.BlockSpec(memory_space=pltpu.SMEM)] + in_vmem(5),
        out_specs=pl.BlockSpec(memory_space=pltpu.VMEM),
        scratch_shapes=[
            pltpu.VMEM((ROWS, count), bf16),
            pltpu.VMEM((2, count, 2 * HD), f32),
            pltpu.VMEM((count, HD), bf16),
        ],
        compiler_params=pltpu.CompilerParams(vmem_limit_bytes=14 * MIB),
        name="attend",
    )(info, qa, qb, keys, values, far)

def merged(in_ref):
    senders = in_ref.shape[0]
    stats = [in_ref[i, HD:, :].astype(f32) for i in range(senders)]
    tops = [s[0:1] for s in stats]
    top = tops[0]
    for other in tops[1:]:
        top = jnp.maximum(top, other)
    out, total = None, None
    for i in range(senders):
        keep = jnp.exp2(tops[i] - top)
        part = in_ref[i, :HD, :].astype(f32) * keep
        part_sum = (stats[i][1:2] + stats[i][2:3]) * keep
        out = part if out is None else out + part
        total = part_sum if total is None else total + part_sum
    return out, top, total

def merge_kernel(in_ref, o_ref):
    message = pack(*merged(in_ref))
    for i in range(o_ref.shape[0]):
        o_ref[i] = message

def merge(came, copies):
    return pl.pallas_call(
        merge_kernel,
        out_shape=jax.ShapeDtypeStruct((copies, ROWS, HD), bf16),
        in_specs=in_vmem(1),
        out_specs=pl.BlockSpec(memory_space=pltpu.VMEM),
        compiler_params=pltpu.CompilerParams(vmem_limit_bytes=4 * MIB),
        name="merge",
    )(came)

def finish_kernel(in_ref, o_ref, turned_ref):
    out, _, total = merged(in_ref)
    turned_ref[...] = (out / total).T
    tokens = o_ref.shape[1]
    heads = [turned_ref[pl.ds(h, tokens, stride=GROUP), :] for h in range(GROUP)]
    rows = jnp.concatenate(heads, axis=1).astype(bf16)
    for i in range(o_ref.shape[0]):
        o_ref[i] = rows

def finish(came, copies):
    return pl.pallas_call(
        finish_kernel,
        out_shape=jax.ShapeDtypeStruct((copies, HD // GROUP, GROUP * HD), bf16),
        in_specs=in_vmem(1),
        out_specs=pl.BlockSpec(memory_space=pltpu.VMEM),
        scratch_shapes=[pltpu.VMEM((HD, HD), f32)],
        compiler_params=pltpu.CompilerParams(vmem_limit_bytes=4 * MIB),
        name="finish",
    )(came)

def project_kernel(a_ref, w_ref, o_ref):
    owners, tokens, depth = a_ref.shape
    rows = a_ref[...].astype(f32).reshape(owners * tokens, depth).astype(bf16)
    out = jnp.dot(rows, w_ref[...], preferred_element_type=f32)
    for x in range(4):
        for zh in range(ZH):
            for zl in range(ZL):
                at = ((x * ZL + zl) * ZH + zh) * 2
                to = (zh % 2) * 8 + zl * 2
                o_ref[x * 2 + zh // 2, to : to + 2, :] = out[at : at + 2]

def project(rows, weight):
    return pl.pallas_call(
        project_kernel,
        out_shape=jax.ShapeDtypeStruct((8, 16, weight.shape[1]), f32),
        in_specs=in_vmem(2),
        out_specs=pl.BlockSpec(memory_space=pltpu.VMEM),
        compiler_params=pltpu.CompilerParams(vmem_limit_bytes=8 * MIB),
        name="project",
    )(rows, weight)


def exchange(parts, axes):
    return lax.all_to_all(parts, axes, split_axis=0, concat_axis=0, tiled=True)


def spread(part, axes, count):
    return exchange(jnp.broadcast_to(part[None], (count,) + part.shape), axes)


def per_device(queries, cache_keys, cache_values, out_weight, cached_length, start):
    count = cache_keys.shape[0]
    x = lax.axis_index(("xa", "xb"))
    z = lax.axis_index(("zh", "zl"))
    depth = ZH * ZL
    near_base, far_base = (x * depth + z) * count, ((3 - x) * depth + z) * count
    info = jnp.stack([x, near_base, far_base, cached_length[0], start[0]]).astype(jnp.int32)
    cache = jnp.concatenate([cache_keys, cache_values], axis=1)
    cache, queries = lax.optimization_barrier((cache, queries))
    far = lax.ppermute(cache, ("xa", "xb"), [(0, 3), (3, 0), (1, 2), (2, 1)])
    own = spread(queries.reshape(2 * GROUP, HD), ("zh", "zl"), depth)
    own = own.reshape(depth * 2 * GROUP, HD)
    other = lax.ppermute(own, "xb", [(0, 1), (1, 0)])
    parts = attend(info, own, other, cache_keys, cache_values, far)
    came = exchange(parts, ("xb", "zl"))
    came = exchange(merge(came, ZH), ("zh",))
    attention = exchange(finish(came, OWNERS), ("xa", "xb", "zl"))
    partial_out = exchange(project(attention, out_weight), ("y", "c"))
    return jnp.sum(partial_out, axis=0).astype(bf16)


def solution(mesh):
    shape = (4, 2, XA, XB, ZH, ZL)
    fine = Mesh(mesh.devices.reshape(shape), ("y", "c", "xa", "xb", "zh", "zl"))
    ctx, kv = ("xa", "xb", "zh", "zl"), ("y", "c")
    return jax.shard_map(
        per_device,
        mesh=fine,
        in_specs=(P(ctx, kv), P(ctx, kv), P(ctx, kv), P(kv, ctx), P(), P()),
        out_specs=P(kv, ctx),
        check_vma=False,
    )
```

```python
import functools
import math

import jax
import jax.numpy as jnp
from jax import lax
from jax.experimental import pallas as pl
from jax.experimental.pallas import tpu as pltpu
from jax.sharding import Mesh
from jax.sharding import PartitionSpec as P

HD = 128
GROUP = 16
SCALE2 = math.log2(math.e) / math.sqrt(HD)
XA, XB, ZH, ZL = 2, 2, 4, 4
OWNERS = XA * XB * ZL
STAT = 16
ROWS = HD + STAT
KEY_BLOCK = 256
HIDDEN = -1e30
LOWEST = -1e5
MIB = 2**20

bf16 = jnp.bfloat16
f32 = jnp.float32
ROW_ROW = (((1,), (1,)), ((), ()))
ROW_COL = (((1,), (0,)), ((), ()))

def in_vmem(count):
    return [pl.BlockSpec(memory_space=pltpu.VMEM)] * count

def pack(out, top, total):
    high = total.astype(bf16).astype(f32)
    blank = jnp.zeros((STAT - 3, out.shape[1]), f32)
    return jnp.concatenate([out, top, high, total - high, blank], axis=0).astype(bf16)

def attend_kernel(info_ref, q_ref, k_ref, v_ref, far_ref, *refs, own):
    if own:
        o_ref, vt_ref, hide_ref, s_ref = refs
    else:
        vt_ref, hide_ref, _, o_ref, s_ref = refs
    near = k_ref.shape[0]
    blocks = 2 * near // KEY_BLOCK
    x, near_base, far_base, cached_end, span_start = [info_ref[i] for i in range(5)]
    owner = x if own else x ^ 1

    def query_rows(zl0):
        parts = []
        for zl in (zl0, zl0 + 1):
            for zh in range(ZH):
                at = (zh * ZL + zl) * 2 * GROUP
                parts.append(q_ref[at : at + 2 * GROUP, :])
        return jnp.concatenate(parts, axis=0)

    def key_rows(block):
        at = block * KEY_BLOCK
        if at < near:
            return k_ref[at : at + KEY_BLOCK, :]
        return far_ref[at - near : at - near + KEY_BLOCK, :HD]

    def hide():
        for half, base in ((0, near_base), (1, far_base)):
            pos = base + lax.broadcasted_iota(jnp.int32, (near, HD), 0)
            token = lax.broadcasted_iota(jnp.int32, (near, HD), 1)
            visible = (pos < cached_end) | (pos >= span_start) & (pos <= span_start + token)
            hidden = jnp.where(visible, 0.0, HIDDEN)
            hide_ref[half * near : (half + 1) * near, :] = hidden.astype(bf16)

    def token_rows(zl0):
        row = lax.broadcasted_iota(jnp.int32, (2 * HD, HD), 0)
        col = lax.broadcasted_iota(jnp.int32, (2 * HD, HD), 1)
        zh, zl, t = (row >> 5) & 3, zl0 + (row >> 7), (row >> 4) & 1
        return jnp.where(owner * 32 + zh * 8 + zl * 2 + t == col, 1.0, 0.0).astype(bf16)

    def score(zl0, slot, masked):
        rows = query_rows(zl0)
        if masked:
            rows = jnp.concatenate([rows, token_rows(zl0)], axis=1)
        top = None
        for block in range(blocks):
            span = slice(block * KEY_BLOCK, (block + 1) * KEY_BLOCK)
            left = key_rows(block)
            if masked:
                left = jnp.concatenate([left, hide_ref[span, :]], axis=1)
            s = lax.dot_general(left, rows, ROW_ROW, preferred_element_type=f32)
            s_ref[slot, span, :] = s
            here = jnp.max(s.reshape(KEY_BLOCK // 8, 8, s.shape[1]), axis=0)
            top = here if top is None else jnp.maximum(top, here)
        top = jnp.max(top, axis=0, keepdims=True) * SCALE2
        return jnp.maximum(top, LOWEST).astype(bf16).astype(f32)

    def weigh(zl0, slot, top):
        total = None
        for block in range(blocks):
            span = slice(block * KEY_BLOCK, (block + 1) * KEY_BLOCK)
            w = jnp.exp2(s_ref[slot, span, :] * SCALE2 - top).astype(bf16)
            part = lax.dot_general(vt_ref[:, span], w, ROW_COL, preferred_element_type=f32)
            total = part if total is None else total + part
        message = pack(total[:HD], top, total[HD : HD + 1])
        to = (owner & 1) * ZL + zl0
        o_ref[to] = message[:, :HD]
        o_ref[to + 1] = message[:, HD:]

    def run(masked):
        if own and masked:
            hide()
        first = score(0, 0, masked)
        if own:
            vt_ref[:HD, :near] = v_ref[...].astype(f32).T.astype(bf16)
            vt_ref[:HD, near:] = far_ref[:, HD:].astype(f32).T.astype(bf16)
            vt_ref[HD:, :] = jnp.ones((STAT, 2 * near), bf16)
        second = score(2, 1, masked)
        weigh(0, 0, first)
        weigh(2, 1, second)

    whole = (near_base + near <= cached_end) & (far_base + near <= cached_end)
    pl.when(whole)(lambda: run(False))
    pl.when(jnp.logical_not(whole))(lambda: run(True))


def attend(info, queries, keys, values, far, earlier=None):
    own = earlier is None
    count = 2 * keys.shape[0]
    message = jax.ShapeDtypeStruct((XB * ZL, ROWS, HD), bf16)
    turned = jax.ShapeDtypeStruct((ROWS, count), bf16)
    hidden = jax.ShapeDtypeStruct((count, HD), bf16)
    operands = [info, queries, keys, values, far]
    if not own:
        parts, turned_values, mask = earlier
        operands += [turned_values, mask, parts]
    return pl.pallas_call(
        functools.partial(attend_kernel, own=own),
        out_shape=(message, turned, hidden) if own else message,
        in_specs=[pl.BlockSpec(memory_space=pltpu.SMEM)] + in_vmem(len(operands) - 1),
        out_specs=tuple(in_vmem(3)) if own else in_vmem(1)[0],
        scratch_shapes=[pltpu.VMEM((2, count, 2 * HD), f32)],
        input_output_aliases={} if own else {7: 0},
        compiler_params=pltpu.CompilerParams(vmem_limit_bytes=14 * MIB),
        cost_estimate=pl.CostEstimate(
            flops=4 * queries.shape[0] * count * HD,
            bytes_accessed=4 * MIB,
            transcendentals=queries.shape[0] * count,
        ),
        name="attend_own" if own else "attend_other",
    )(*operands)


def merged(in_ref):
    senders = in_ref.shape[0]
    stats = [in_ref[i, HD:, :].astype(f32) for i in range(senders)]
    tops = [s[0:1] for s in stats]
    top = tops[0]
    for other in tops[1:]:
        top = jnp.maximum(top, other)
    out, total = None, None
    for i in range(senders):
        keep = jnp.exp2(tops[i] - top)
        part = in_ref[i, :HD, :].astype(f32) * keep
        part_sum = (stats[i][1:2] + stats[i][2:3]) * keep
        out = part if out is None else out + part
        total = part_sum if total is None else total + part_sum
    return out, top, total

def merge_kernel(in_ref, o_ref):
    message = pack(*merged(in_ref))
    for i in range(o_ref.shape[0]):
        o_ref[i] = message

def merge(came, copies):
    return pl.pallas_call(
        merge_kernel,
        out_shape=jax.ShapeDtypeStruct((copies, ROWS, HD), bf16),
        in_specs=in_vmem(1),
        out_specs=pl.BlockSpec(memory_space=pltpu.VMEM),
        compiler_params=pltpu.CompilerParams(vmem_limit_bytes=4 * MIB),
        name="merge",
    )(came)

def finish_kernel(in_ref, o_ref, turned_ref):
    out, _, total = merged(in_ref)
    turned_ref[...] = (out / total).T
    tokens = o_ref.shape[1]
    heads = [turned_ref[pl.ds(h, tokens, stride=GROUP), :] for h in range(GROUP)]
    rows = jnp.concatenate(heads, axis=1).astype(bf16)
    for i in range(o_ref.shape[0]):
        o_ref[i] = rows

def finish(came, copies):
    return pl.pallas_call(
        finish_kernel,
        out_shape=jax.ShapeDtypeStruct((copies, HD // GROUP, GROUP * HD), bf16),
        in_specs=in_vmem(1),
        out_specs=pl.BlockSpec(memory_space=pltpu.VMEM),
        scratch_shapes=[pltpu.VMEM((HD, HD), f32)],
        compiler_params=pltpu.CompilerParams(vmem_limit_bytes=4 * MIB),
        name="finish",
    )(came)

def project_kernel(a_ref, w_ref, o_ref):
    owners, tokens, depth = a_ref.shape
    rows = a_ref[...].astype(f32).reshape(owners * tokens, depth).astype(bf16)
    out = jnp.dot(rows, w_ref[...], preferred_element_type=f32)
    for x in range(4):
        for zh in range(ZH):
            for zl in range(ZL):
                at = ((x * ZL + zl) * ZH + zh) * 2
                to = (zh % 2) * 8 + zl * 2
                o_ref[x * 2 + zh // 2, to : to + 2, :] = out[at : at + 2]

def project(rows, weight):
    return pl.pallas_call(
        project_kernel,
        out_shape=jax.ShapeDtypeStruct((8, 16, weight.shape[1]), f32),
        in_specs=in_vmem(2),
        out_specs=pl.BlockSpec(memory_space=pltpu.VMEM),
        compiler_params=pltpu.CompilerParams(vmem_limit_bytes=8 * MIB),
        name="project",
    )(rows, weight)


def exchange(parts, axes):
    return lax.all_to_all(parts, axes, split_axis=0, concat_axis=0, tiled=True)


def spread(part, axes, count):
    return exchange(jnp.broadcast_to(part[None], (count,) + part.shape), axes)


def per_device(queries, cache_keys, cache_values, out_weight, cached_length, start):
    count = cache_keys.shape[0]
    x = lax.axis_index(("xa", "xb"))
    z = lax.axis_index(("zh", "zl"))
    depth = ZH * ZL
    near_base, far_base = (x * depth + z) * count, ((3 - x) * depth + z) * count
    info = jnp.stack([x, near_base, far_base, cached_length[0], start[0]]).astype(jnp.int32)
    cache = jnp.concatenate([cache_keys, cache_values], axis=1)
    cache, queries = lax.optimization_barrier((cache, queries))
    far = lax.ppermute(cache, ("xa", "xb"), [(0, 3), (3, 0), (1, 2), (2, 1)])
    own = spread(queries.reshape(2 * GROUP, HD), ("zh", "zl"), depth)
    own = own.reshape(depth * 2 * GROUP, HD)
    other = lax.ppermute(own, "xb", [(0, 1), (1, 0)])
    earlier = attend(info, own, cache_keys, cache_values, far)
    parts = attend(info, other, cache_keys, cache_values, far, earlier)
    came = exchange(parts, ("xb", "zl"))
    came = exchange(merge(came, ZH), ("zh",))
    attention = exchange(finish(came, OWNERS), ("xa", "xb", "zl"))
    partial_out = exchange(project(attention, out_weight), ("y", "c"))
    return jnp.sum(partial_out, axis=0).astype(bf16)


def solution(mesh):
    shape = (4, 2, XA, XB, ZH, ZL)
    fine = Mesh(mesh.devices.reshape(shape), ("y", "c", "xa", "xb", "zh", "zl"))
    ctx, kv = ("xa", "xb", "zh", "zl"), ("y", "c")
    return jax.shard_map(
        per_device,
        mesh=fine,
        in_specs=(P(ctx, kv), P(ctx, kv), P(ctx, kv), P(kv, ctx), P(), P()),
        out_specs=P(kv, ctx),
        check_vma=False,
    )
```

```python
import math

import jax
import jax.numpy as jnp
from jax import lax
from jax.experimental import pallas as pl
from jax.experimental.pallas import tpu as pltpu
from jax.sharding import Mesh
from jax.sharding import PartitionSpec as P

HD = 128
GROUP = 16
SCALE2 = math.log2(math.e) / math.sqrt(HD)
XA, XB, ZH, ZL = 2, 2, 4, 4
STAT = 16
ROWS = HD + STAT
KEY_BLOCK = 256
HIDDEN = -1e30
LOWEST = -1e5
MIB = 2**20

bf16 = jnp.bfloat16
f32 = jnp.float32
ROW_ROW = (((1,), (1,)), ((), ()))
ROW_COL = (((1,), (0,)), ((), ()))

def in_vmem(count):
    return [pl.BlockSpec(memory_space=pltpu.VMEM)] * count

def pack(out, top, total):
    high = total.astype(bf16).astype(f32)
    blank = jnp.zeros((STAT - 3, out.shape[1]), f32)
    return jnp.concatenate([out, top, high, total - high, blank], axis=0).astype(bf16)

def attend_kernel(info_ref, qa_ref, qb_ref, k_ref, v_ref, kv_ref, o_ref, vt_ref, s_ref, hide_ref):
    near = k_ref.shape[0]
    keys = 2 * near
    blocks = keys // KEY_BLOCK
    x, near_base, far_base, cached_end, span_start = [info_ref[i] for i in range(5)]
    vt_ref[:HD, :near] = v_ref[...].astype(f32).T.astype(bf16)
    vt_ref[:HD, near:] = kv_ref[:, HD:].astype(f32).T.astype(bf16)
    vt_ref[HD:, :] = jnp.ones((STAT, keys), bf16)

    def query_rows(zl):
        parts = []
        for t in range(2):
            for ref in (qa_ref, qb_ref):
                for zh in range(ZH):
                    at = ((zh * ZL + zl) * 2 + t) * GROUP
                    parts.append(ref[at : at + GROUP, :])
        return jnp.concatenate(parts, axis=0)

    def key_rows(block):
        at = block * KEY_BLOCK
        if at < near:
            return k_ref[at : at + KEY_BLOCK, :]
        return kv_ref[at - near : at - near + KEY_BLOCK, :HD]

    def hide():
        for half, base in ((0, near_base), (1, far_base)):
            pos = base + lax.broadcasted_iota(jnp.int32, (near, HD), 0)
            token = lax.broadcasted_iota(jnp.int32, (near, HD), 1)
            visible = (pos < cached_end) | (pos >= span_start) & (pos <= span_start + token)
            hide_ref[half * near : (half + 1) * near, :] = jnp.where(visible, 0.0, HIDDEN).astype(bf16)

    def token_rows(zl):
        row = lax.broadcasted_iota(jnp.int32, (2 * HD, HD), 0)
        col = lax.broadcasted_iota(jnp.int32, (2 * HD, HD), 1)
        t, owner, zh = row >> 7, x ^ ((row >> 6) & 1), (row >> 4) & 3
        return jnp.where(owner * 32 + zh * 8 + zl * 2 + t == col, 1.0, 0.0).astype(bf16)

    def score(i, masked):
        rows = query_rows(i)
        if masked:
            rows = jnp.concatenate([rows, token_rows(i)], axis=1)
        top = None
        for block in range(blocks):
            span = slice(block * KEY_BLOCK, (block + 1) * KEY_BLOCK)
            left = key_rows(block)
            if masked:
                left = jnp.concatenate([left, hide_ref[span, :]], axis=1)
            s = lax.dot_general(left, rows, ROW_ROW, preferred_element_type=f32)
            s_ref[i % 2, span, :] = s
            here = jnp.max(s.reshape(KEY_BLOCK // 8, 8, s.shape[1]), axis=0)
            top = here if top is None else jnp.maximum(top, here)
        top = jnp.max(top, axis=0, keepdims=True) * SCALE2
        return jnp.maximum(top, LOWEST).astype(bf16).astype(f32)

    def weigh(i, top):
        total = None
        for block in range(blocks):
            span = slice(block * KEY_BLOCK, (block + 1) * KEY_BLOCK)
            w = jnp.exp2(s_ref[i % 2, span, :] * SCALE2 - top).astype(bf16)
            part = lax.dot_general(vt_ref[:, span], w, ROW_COL, preferred_element_type=f32)
            total = part if total is None else total + part
        message = pack(total[:HD], top, total[HD : HD + 1])
        o_ref[i] = message[:, :HD]
        o_ref[ZL + i] = message[:, HD:]

    def run(masked):
        if masked:
            hide()
        top = score(0, masked)
        for i in range(ZL):
            following = score(i + 1, masked) if i + 1 < ZL else None
            weigh(i, top)
            top = following
    whole = (near_base + near <= cached_end) & (far_base + near <= cached_end)
    pl.when(whole)(lambda: run(False))
    pl.when(jnp.logical_not(whole))(lambda: run(True))

def attend(info, qa, qb, keys, values, far):
    count = 2 * keys.shape[0]
    return pl.pallas_call(
        attend_kernel,
        out_shape=jax.ShapeDtypeStruct((XB * ZL, ROWS, HD), bf16),
        in_specs=[pl.BlockSpec(memory_space=pltpu.SMEM)] + in_vmem(5),
        out_specs=pl.BlockSpec(memory_space=pltpu.VMEM),
        scratch_shapes=[
            pltpu.VMEM((ROWS, count), bf16),
            pltpu.VMEM((2, count, 2 * HD), f32),
            pltpu.VMEM((count, HD), bf16),
        ],
        compiler_params=pltpu.CompilerParams(vmem_limit_bytes=14 * MIB),
        name="attend",
    )(info, qa, qb, keys, values, far)

def merged(messages):
    tops = [m[HD : HD + 1] for m in messages]
    top = tops[0]
    for other in tops[1:]:
        top = jnp.maximum(top, other)
    out, total = None, None
    for m, own in zip(messages, tops):
        keep = jnp.exp2(own - top)
        part, part_sum = m[:HD] * keep, (m[HD + 1 : HD + 2] + m[HD + 2 : HD + 3]) * keep
        out = part if out is None else out + part
        total = part_sum if total is None else total + part_sum
    return out, top, total


def merge_kernel(in_ref, o_ref):
    messages = [in_ref[i].astype(f32) for i in range(XB * ZL)]
    half = HD // 2
    for i in range(ZL, XB * ZL):
        messages[i] = jnp.concatenate([messages[i][:, half:], messages[i][:, :half]], axis=1)
    message = pack(*merged(messages))
    for i in range(o_ref.shape[0]):
        o_ref[i] = message

def merge(came, copies):
    return pl.pallas_call(
        merge_kernel,
        out_shape=jax.ShapeDtypeStruct((copies, ROWS, HD), bf16),
        in_specs=in_vmem(1),
        out_specs=pl.BlockSpec(memory_space=pltpu.VMEM),
        compiler_params=pltpu.CompilerParams(vmem_limit_bytes=4 * MIB),
        name="merge",
    )(came)

def finish_kernel(in_ref, o_ref, turned_ref):
    out, _, total = merged([in_ref[i].astype(f32) for i in range(in_ref.shape[0])])
    turned_ref[...] = (out / total).T
    tokens = o_ref.shape[1]
    heads = [turned_ref[pl.ds(h, tokens, stride=GROUP), :] for h in range(GROUP)]
    rows = jnp.concatenate(heads, axis=1).astype(bf16)
    for i in range(o_ref.shape[0]):
        o_ref[i] = rows

def finish(came, copies):
    return pl.pallas_call(
        finish_kernel,
        out_shape=jax.ShapeDtypeStruct((copies, HD // GROUP, GROUP * HD), bf16),
        in_specs=in_vmem(1),
        out_specs=pl.BlockSpec(memory_space=pltpu.VMEM),
        scratch_shapes=[pltpu.VMEM((HD, HD), f32)],
        compiler_params=pltpu.CompilerParams(vmem_limit_bytes=4 * MIB),
        name="finish",
    )(came)

def project_kernel(info_ref, a_ref, own_ref, other_ref, o_ref):
    senders, tokens, depth = a_ref.shape
    xb = info_ref[0] & 1
    rows = a_ref[...].astype(f32).reshape(senders * tokens, depth).astype(bf16)
    for to, w_ref in ((xb, own_ref), (1 - xb, other_ref)):
        out = jnp.dot(rows, w_ref[...], preferred_element_type=f32)
        for x in range(XA * XB):
            for half in range(2):
                parts = []
                for zl in range(ZL):
                    at = (x // XB * ZL + zl) * tokens + x % XB * ZH + half * 2
                    parts.append(out[at : at + 2])
                o_ref[(x * 2 + half) * XB + to] = jnp.concatenate(parts, axis=0)


def project(info, rows, weight, other):
    return pl.pallas_call(
        project_kernel,
        out_shape=jax.ShapeDtypeStruct((8 * XB, 8, weight.shape[1]), f32),
        in_specs=[pl.BlockSpec(memory_space=pltpu.SMEM)] + in_vmem(3),
        out_specs=pl.BlockSpec(memory_space=pltpu.VMEM),
        compiler_params=pltpu.CompilerParams(vmem_limit_bytes=8 * MIB),
        name="project",
    )(info, rows, weight, other)


def total_kernel(in_ref, o_ref, s_ref):
    for t in range(2):
        out = in_ref[t]
        for sender in range(XB + t, in_ref.shape[0], XB):
            out = out + in_ref[sender]
        for zl in range(ZL):
            for zh in range(2):
                to = (zh * ZL + zl) * 2 + t
                s_ref[to : to + 1, :] = out[zl * 2 + zh : zl * 2 + zh + 1]
    o_ref[...] = s_ref[...].astype(bf16)


def total(came):
    columns = came.shape[2]
    return pl.pallas_call(
        total_kernel,
        out_shape=jax.ShapeDtypeStruct((16, columns), bf16),
        in_specs=in_vmem(1),
        out_specs=pl.BlockSpec(memory_space=pltpu.VMEM),
        scratch_shapes=[pltpu.VMEM((16, columns), f32)],
        compiler_params=pltpu.CompilerParams(vmem_limit_bytes=2 * MIB),
        name="total",
    )(came)


def exchange(parts, axes):
    return lax.all_to_all(parts, axes, split_axis=0, concat_axis=0, tiled=True)


def spread(part, axes, count):
    return exchange(jnp.broadcast_to(part[None], (count,) + part.shape), axes)


def per_device(queries, cache_keys, cache_values, out_weight, cached_length, start):
    count = cache_keys.shape[0]
    x = lax.axis_index(("xa", "xb"))
    z = lax.axis_index(("zh", "zl"))
    depth = ZH * ZL
    near_base, far_base = (x * depth + z) * count, ((3 - x) * depth + z) * count
    info = jnp.stack([x, near_base, far_base, cached_length[0], start[0]]).astype(jnp.int32)
    cache = jnp.concatenate([cache_keys, cache_values], axis=1)
    cache, queries = lax.optimization_barrier((cache, queries))
    far = lax.ppermute(cache, ("xa", "xb"), [(0, 3), (3, 0), (1, 2), (2, 1)])
    own = spread(queries.reshape(2 * GROUP, HD), ("zh", "zl"), depth)
    own = own.reshape(depth * 2 * GROUP, HD)
    swap = [(0, 1), (1, 0)]
    other = lax.ppermute(own, "xb", swap)
    other_weight = lax.ppermute(out_weight, "xb", swap)
    parts = attend(info, own, other, cache_keys, cache_values, far)
    came = exchange(parts, ("xb", "zl"))
    came = exchange(merge(came, ZH), ("zh",))
    attention = exchange(finish(came, XA * ZL), ("xa", "zl"))
    partial_out = exchange(project(info, attention, out_weight, other_weight), ("y", "c", "xb"))
    return total(partial_out)


def solution(mesh):
    shape = (4, 2, XA, XB, ZH, ZL)
    fine = Mesh(mesh.devices.reshape(shape), ("y", "c", "xa", "xb", "zh", "zl"))
    ctx, kv = ("xa", "xb", "zh", "zl"), ("y", "c")
    return jax.shard_map(
        per_device,
        mesh=fine,
        in_specs=(P(ctx, kv), P(ctx, kv), P(ctx, kv), P(kv, ctx), P(), P()),
        out_specs=P(kv, ctx),
        check_vma=False,
    )
```

```python
import math

import jax
import jax.numpy as jnp
from jax import lax
from jax.experimental import pallas as pl
from jax.experimental.pallas import tpu as pltpu
from jax.sharding import Mesh
from jax.sharding import PartitionSpec as P

HD = 128
GROUP = 16
SCALE2 = math.log2(math.e) / math.sqrt(HD)
XA, XB, ZH, ZL = 2, 2, 4, 4
STAT = 16
ROWS = HD + STAT
KEY_BLOCK = 256
HIDDEN = -1e30
LOWEST = -1e5
MIB = 2**20

bf16 = jnp.bfloat16
f32 = jnp.float32
ROW_ROW = (((1,), (1,)), ((), ()))
ROW_COL = (((1,), (0,)), ((), ()))

def in_vmem(count):
    return [pl.BlockSpec(memory_space=pltpu.VMEM)] * count

def pack(out, top, total):
    high = total.astype(bf16).astype(f32)
    blank = jnp.zeros((STAT - 3, out.shape[1]), f32)
    return jnp.concatenate([out, top, high, total - high, blank], axis=0).astype(bf16)

def attend_kernel(
    info_ref, qa_ref, qb_ref, k_ref, v_ref, far_ref, o_ref, vt_ref, s_ref, hide_ref, kv_ref, sem
):
    near = k_ref.shape[0]
    keys = 2 * near
    blocks = keys // KEY_BLOCK
    x, near_base, far_base, cached_end, span_start = [info_ref[i] for i in range(5)]
    vt_ref[:HD, :near] = v_ref[...].astype(f32).T.astype(bf16)
    vt_ref[HD:, :] = jnp.ones((STAT, keys), bf16)
    fetch = pltpu.make_async_copy(far_ref, kv_ref, sem)
    fetch.start()

    def query_rows(zl):
        parts = []
        for t in range(2):
            for ref in (qa_ref, qb_ref):
                for zh in range(ZH):
                    at = ((zh * ZL + zl) * 2 + t) * GROUP
                    parts.append(ref[at : at + GROUP, :])
        return jnp.concatenate(parts, axis=0)

    def key_rows(block):
        at = block * KEY_BLOCK
        if at < near:
            return k_ref[at : at + KEY_BLOCK, :]
        return kv_ref[at - near : at - near + KEY_BLOCK, :HD]

    def hide():
        for half, base in ((0, near_base), (1, far_base)):
            pos = base + lax.broadcasted_iota(jnp.int32, (near, HD), 0)
            token = lax.broadcasted_iota(jnp.int32, (near, HD), 1)
            visible = (pos < cached_end) | (pos >= span_start) & (pos <= span_start + token)
            hide_ref[half * near : (half + 1) * near, :] = jnp.where(visible, 0.0, HIDDEN).astype(bf16)

    def token_rows(zl):
        row = lax.broadcasted_iota(jnp.int32, (2 * HD, HD), 0)
        col = lax.broadcasted_iota(jnp.int32, (2 * HD, HD), 1)
        t, owner, zh = row >> 7, x ^ ((row >> 6) & 1), (row >> 4) & 3
        return jnp.where(owner * 32 + zh * 8 + zl * 2 + t == col, 1.0, 0.0).astype(bf16)

    def score(i, masked):
        rows = query_rows(i)
        if masked:
            rows = jnp.concatenate([rows, token_rows(i)], axis=1)
        top = None
        for block in range(blocks):
            span = slice(block * KEY_BLOCK, (block + 1) * KEY_BLOCK)
            if i == 0 and block * KEY_BLOCK == near:
                fetch.wait()
                vt_ref[:HD, near:] = kv_ref[:, HD:].astype(f32).T.astype(bf16)
            left = key_rows(block)
            if masked:
                left = jnp.concatenate([left, hide_ref[span, :]], axis=1)
            s = lax.dot_general(left, rows, ROW_ROW, preferred_element_type=f32)
            s_ref[i % 2, span, :] = s
            here = jnp.max(s.reshape(KEY_BLOCK // 8, 8, s.shape[1]), axis=0)
            top = here if top is None else jnp.maximum(top, here)
        top = jnp.max(top, axis=0, keepdims=True) * SCALE2
        return jnp.maximum(top, LOWEST).astype(bf16).astype(f32)

    def weigh(i, top):
        total = None
        for block in range(blocks):
            span = slice(block * KEY_BLOCK, (block + 1) * KEY_BLOCK)
            w = jnp.exp2(s_ref[i % 2, span, :] * SCALE2 - top).astype(bf16)
            part = lax.dot_general(vt_ref[:, span], w, ROW_COL, preferred_element_type=f32)
            total = part if total is None else total + part
        message = pack(total[:HD], top, total[HD : HD + 1])
        o_ref[i] = message[:, :HD]
        o_ref[ZL + i] = message[:, HD:]

    def run(masked):
        if masked:
            hide()
        top = score(0, masked)
        for i in range(ZL):
            following = score(i + 1, masked) if i + 1 < ZL else None
            weigh(i, top)
            top = following
    whole = (near_base + near <= cached_end) & (far_base + near <= cached_end)
    pl.when(whole)(lambda: run(False))
    pl.when(jnp.logical_not(whole))(lambda: run(True))

def attend(info, qa, qb, keys, values, far):
    count = 2 * keys.shape[0]
    return pl.pallas_call(
        attend_kernel,
        out_shape=jax.ShapeDtypeStruct((XB * ZL, ROWS, HD), bf16),
        in_specs=[pl.BlockSpec(memory_space=pltpu.SMEM)]
        + in_vmem(4)
        + [pl.BlockSpec(memory_space=pl.ANY)],
        out_specs=pl.BlockSpec(memory_space=pltpu.VMEM),
        scratch_shapes=[
            pltpu.VMEM((ROWS, count), bf16),
            pltpu.VMEM((2, count, 2 * HD), f32),
            pltpu.VMEM((count, HD), bf16),
            pltpu.VMEM(far.shape, bf16),
            pltpu.SemaphoreType.DMA,
        ],
        compiler_params=pltpu.CompilerParams(vmem_limit_bytes=16 * MIB),
        name="attend",
    )(info, qa, qb, keys, values, far)

def merged(messages):
    tops = [m[HD : HD + 1] for m in messages]
    top = tops[0]
    for other in tops[1:]:
        top = jnp.maximum(top, other)
    out, total = None, None
    for m, own in zip(messages, tops):
        keep = jnp.exp2(own - top)
        part, part_sum = m[:HD] * keep, (m[HD + 1 : HD + 2] + m[HD + 2 : HD + 3]) * keep
        out = part if out is None else out + part
        total = part_sum if total is None else total + part_sum
    return out, top, total


def merge_kernel(in_ref, o_ref):
    messages = [in_ref[i].astype(f32) for i in range(XB * ZL)]
    half = HD // 2
    for i in range(ZL, XB * ZL):
        messages[i] = jnp.concatenate([messages[i][:, half:], messages[i][:, :half]], axis=1)
    message = pack(*merged(messages))
    for i in range(o_ref.shape[0]):
        o_ref[i] = message

def merge(came, copies):
    return pl.pallas_call(
        merge_kernel,
        out_shape=jax.ShapeDtypeStruct((copies, ROWS, HD), bf16),
        in_specs=in_vmem(1),
        out_specs=pl.BlockSpec(memory_space=pltpu.VMEM),
        compiler_params=pltpu.CompilerParams(vmem_limit_bytes=4 * MIB),
        name="merge",
    )(came)

def finish_kernel(in_ref, o_ref, turned_ref):
    out, _, total = merged([in_ref[i].astype(f32) for i in range(in_ref.shape[0])])
    turned_ref[...] = (out / total).T
    tokens = o_ref.shape[1]
    heads = [turned_ref[pl.ds(h, tokens, stride=GROUP), :] for h in range(GROUP)]
    rows = jnp.concatenate(heads, axis=1).astype(bf16)
    for i in range(o_ref.shape[0]):
        o_ref[i] = rows

def finish(came, copies):
    return pl.pallas_call(
        finish_kernel,
        out_shape=jax.ShapeDtypeStruct((copies, HD // GROUP, GROUP * HD), bf16),
        in_specs=in_vmem(1),
        out_specs=pl.BlockSpec(memory_space=pltpu.VMEM),
        scratch_shapes=[pltpu.VMEM((HD, HD), f32)],
        compiler_params=pltpu.CompilerParams(vmem_limit_bytes=4 * MIB),
        name="finish",
    )(came)

def project_kernel(info_ref, a_ref, own_ref, other_ref, o_ref):
    senders, tokens, depth = a_ref.shape
    xb = info_ref[0] & 1
    rows = a_ref[...].astype(f32).reshape(senders * tokens, depth).astype(bf16)
    for to, w_ref in ((xb, own_ref), (1 - xb, other_ref)):
        out = jnp.dot(rows, w_ref[...], preferred_element_type=f32)
        for x in range(XA * XB):
            for half in range(2):
                parts = []
                for zl in range(ZL):
                    at = (x // XB * ZL + zl) * tokens + x % XB * ZH + half * 2
                    parts.append(out[at : at + 2])
                o_ref[(x * 2 + half) * XB + to] = jnp.concatenate(parts, axis=0)


def project(info, rows, weight, other):
    return pl.pallas_call(
        project_kernel,
        out_shape=jax.ShapeDtypeStruct((8 * XB, 8, weight.shape[1]), f32),
        in_specs=[pl.BlockSpec(memory_space=pltpu.SMEM)] + in_vmem(3),
        out_specs=pl.BlockSpec(memory_space=pltpu.VMEM),
        compiler_params=pltpu.CompilerParams(vmem_limit_bytes=8 * MIB),
        name="project",
    )(info, rows, weight, other)


def total_kernel(in_ref, o_ref, s_ref):
    for t in range(2):
        out = in_ref[t]
        for sender in range(XB + t, in_ref.shape[0], XB):
            out = out + in_ref[sender]
        for zl in range(ZL):
            for zh in range(2):
                to = (zh * ZL + zl) * 2 + t
                s_ref[to : to + 1, :] = out[zl * 2 + zh : zl * 2 + zh + 1]
    o_ref[...] = s_ref[...].astype(bf16)


def total(came):
    columns = came.shape[2]
    return pl.pallas_call(
        total_kernel,
        out_shape=jax.ShapeDtypeStruct((16, columns), bf16),
        in_specs=in_vmem(1),
        out_specs=pl.BlockSpec(memory_space=pltpu.VMEM),
        scratch_shapes=[pltpu.VMEM((16, columns), f32)],
        compiler_params=pltpu.CompilerParams(vmem_limit_bytes=2 * MIB),
        name="total",
    )(came)


def exchange(parts, axes):
    return lax.all_to_all(parts, axes, split_axis=0, concat_axis=0, tiled=True)


def spread(part, axes, count):
    return exchange(jnp.broadcast_to(part[None], (count,) + part.shape), axes)


def per_device(queries, cache_keys, cache_values, out_weight, cached_length, start):
    count = cache_keys.shape[0]
    x = lax.axis_index(("xa", "xb"))
    z = lax.axis_index(("zh", "zl"))
    depth = ZH * ZL
    near_base, far_base = (x * depth + z) * count, ((3 - x) * depth + z) * count
    info = jnp.stack([x, near_base, far_base, cached_length[0], start[0]]).astype(jnp.int32)
    cache = jnp.concatenate([cache_keys, cache_values], axis=1)
    cache, queries = lax.optimization_barrier((cache, queries))
    far = lax.ppermute(cache, ("xa", "xb"), [(0, 3), (3, 0), (1, 2), (2, 1)])
    own = spread(queries.reshape(2 * GROUP, HD), ("zh", "zl"), depth)
    own = own.reshape(depth * 2 * GROUP, HD)
    swap = [(0, 1), (1, 0)]
    other = lax.ppermute(own, "xb", swap)
    other_weight = lax.ppermute(out_weight, "xb", swap)
    parts = attend(info, own, other, cache_keys, cache_values, far)
    came = exchange(parts, ("xb", "zl"))
    came, other_weight = lax.optimization_barrier((came, other_weight))
    came = exchange(merge(came, ZH), ("zh",))
    attention = exchange(finish(came, XA * ZL), ("xa", "zl"))
    partial_out = exchange(project(info, attention, out_weight, other_weight), ("y", "c", "xb"))
    return total(partial_out)


def solution(mesh):
    shape = (4, 2, XA, XB, ZH, ZL)
    fine = Mesh(mesh.devices.reshape(shape), ("y", "c", "xa", "xb", "zh", "zl"))
    ctx, kv = ("xa", "xb", "zh", "zl"), ("y", "c")
    return jax.shard_map(
        per_device,
        mesh=fine,
        in_specs=(P(ctx, kv), P(ctx, kv), P(ctx, kv), P(kv, ctx), P(), P()),
        out_specs=P(kv, ctx),
        check_vma=False,
    )
```

```python
import math

import jax
import jax.numpy as jnp
from jax import lax
from jax.experimental import pallas as pl
from jax.experimental.pallas import tpu as pltpu
from jax.sharding import Mesh
from jax.sharding import PartitionSpec as P

HD = 128
GROUP = 16
SCALE2 = math.log2(math.e) / math.sqrt(HD)
X, ZH, ZL = 4, 4, 4
OWNERS = X * ZL
STAT = 16
ROWS = HD + STAT
KEY_BLOCK = 256
HIDDEN = -1e30
LOWEST = -1e5
MIB = 2**20
SHARE = [(x, x ^ 1) for x in range(X)] + [(X + x, X + 3 - x) for x in range(X)]
SWAP = [(x, 3 - x) for x in range(X)] + [(X + x, X + (x ^ 1)) for x in range(X)]
OWNER_GROUPS = [
    [(c * X + x) * ZL + zl for x in xs for zl in range(ZL)]
    for c, xs in ((0, (0, 1)), (0, (2, 3)), (1, (0, 3)), (1, (1, 2)))
]

bf16 = jnp.bfloat16
f32 = jnp.float32
ROW_ROW = (((1,), (1,)), ((), ()))
ROW_COL = (((1,), (0,)), ((), ()))

def in_vmem(count):
    return [pl.BlockSpec(memory_space=pltpu.VMEM)] * count

def pack(out, top, total):
    high = total.astype(bf16).astype(f32)
    blank = jnp.zeros((STAT - 3, out.shape[1]), f32)
    return jnp.concatenate([out, top, high, total - high, blank], axis=0).astype(bf16)

def attend_kernel(
    info_ref, qa_ref, qb_ref, k_ref, v_ref, kf_ref, vf_ref, o_ref, vt_ref, s_ref, hide_ref
):
    near = k_ref.shape[0]
    keys = 2 * near
    blocks = keys // KEY_BLOCK
    x, pair, rank, near_base, far_base, cached_end, span_start = [info_ref[i] for i in range(7)]
    vt_ref[:HD, :near] = v_ref[...].astype(f32).T.astype(bf16)
    vt_ref[:HD, near:] = vf_ref[...].astype(f32).T.astype(bf16)
    vt_ref[HD:, :] = jnp.ones((STAT, keys), bf16)
    chunks = [(q, zl) for q in (0, 1) for zl in range(0, ZL, 2)]

    def query_rows(chunk):
        q, zl0 = chunk
        ref = (qa_ref, qb_ref)[q]
        parts = []
        for zl in (zl0, zl0 + 1):
            for zh in range(ZH):
                at = (zh * ZL + zl) * 2 * GROUP
                parts.append(ref[at : at + 2 * GROUP, :])
        return jnp.concatenate(parts, axis=0)

    def key_rows(block):
        at = block * KEY_BLOCK
        if at < near:
            return k_ref[at : at + KEY_BLOCK, :]
        return kf_ref[at - near : at - near + KEY_BLOCK, :]

    def hide():
        for half, base in ((0, near_base), (1, far_base)):
            pos = base + lax.broadcasted_iota(jnp.int32, (near, HD), 0)
            token = lax.broadcasted_iota(jnp.int32, (near, HD), 1)
            visible = (pos < cached_end) | (pos >= span_start) & (pos <= span_start + token)
            hide_ref[half * near : (half + 1) * near, :] = jnp.where(visible, 0.0, HIDDEN).astype(bf16)

    def token_rows(chunk):
        q, zl0 = chunk
        row = lax.broadcasted_iota(jnp.int32, (2 * HD, HD), 0)
        col = lax.broadcasted_iota(jnp.int32, (2 * HD, HD), 1)
        owner = x if q == 0 else pair
        token = owner * 32 + ((row >> 5) & 3) * 8 + (zl0 + (row >> 7)) * 2 + ((row >> 4) & 1)
        return jnp.where(token == col, 1.0, 0.0).astype(bf16)

    def score(i, masked):
        rows = query_rows(chunks[i])
        if masked:
            rows = jnp.concatenate([rows, token_rows(chunks[i])], axis=1)
        top = None
        for block in range(blocks):
            span = slice(block * KEY_BLOCK, (block + 1) * KEY_BLOCK)
            left = key_rows(block)
            if masked:
                left = jnp.concatenate([left, hide_ref[span, :]], axis=1)
            s = lax.dot_general(left, rows, ROW_ROW, preferred_element_type=f32)
            s_ref[i % 2, span, :] = s
            here = jnp.max(s.reshape(KEY_BLOCK // 8, 8, s.shape[1]), axis=0)
            top = here if top is None else jnp.maximum(top, here)
        top = jnp.max(top, axis=0, keepdims=True) * SCALE2
        return jnp.maximum(top, LOWEST).astype(bf16).astype(f32)

    def weigh(i, top):
        total = None
        for block in range(blocks):
            span = slice(block * KEY_BLOCK, (block + 1) * KEY_BLOCK)
            w = jnp.exp2(s_ref[i % 2, span, :] * SCALE2 - top).astype(bf16)
            part = lax.dot_general(vt_ref[:, span], w, ROW_COL, preferred_element_type=f32)
            total = part if total is None else total + part
        message = pack(total[:HD], top, total[HD : HD + 1])
        q, zl = chunks[i]
        to = (rank if q == 0 else 1 - rank) * ZL + zl
        o_ref[to] = message[:, :HD]
        o_ref[to + 1] = message[:, HD:]

    def run(masked):
        if masked:
            hide()
        top = score(0, masked)
        for i in range(len(chunks)):
            following = score(i + 1, masked) if i + 1 < len(chunks) else None
            weigh(i, top)
            top = following
    whole = (near_base + near <= cached_end) & (far_base + near <= cached_end)
    pl.when(whole)(lambda: run(False))
    pl.when(jnp.logical_not(whole))(lambda: run(True))

def attend(info, qa, qb, keys, values, far_keys, far_values):
    count = 2 * keys.shape[0]
    return pl.pallas_call(
        attend_kernel,
        out_shape=jax.ShapeDtypeStruct((2 * ZL, ROWS, HD), bf16),
        in_specs=[pl.BlockSpec(memory_space=pltpu.SMEM)] + in_vmem(6),
        out_specs=pl.BlockSpec(memory_space=pltpu.VMEM),
        scratch_shapes=[
            pltpu.VMEM((ROWS, count), bf16),
            pltpu.VMEM((2, count, 2 * HD), f32),
            pltpu.VMEM((count, HD), bf16),
        ],
        compiler_params=pltpu.CompilerParams(vmem_limit_bytes=14 * MIB),
        name="attend",
    )(info, qa, qb, keys, values, far_keys, far_values)

def merged(in_ref):
    senders = in_ref.shape[0]
    stats = [in_ref[i, HD:, :].astype(f32) for i in range(senders)]
    tops = [s[0:1] for s in stats]
    top = tops[0]
    for other in tops[1:]:
        top = jnp.maximum(top, other)
    out, total = None, None
    for i in range(senders):
        keep = jnp.exp2(tops[i] - top)
        part = in_ref[i, :HD, :].astype(f32) * keep
        part_sum = (stats[i][1:2] + stats[i][2:3]) * keep
        out = part if out is None else out + part
        total = part_sum if total is None else total + part_sum
    return out, top, total

def merge_kernel(in_ref, o_ref):
    message = pack(*merged(in_ref))
    for i in range(o_ref.shape[0]):
        o_ref[i] = message

def merge(came, copies):
    return pl.pallas_call(
        merge_kernel,
        out_shape=jax.ShapeDtypeStruct((copies, ROWS, HD), bf16),
        in_specs=in_vmem(1),
        out_specs=pl.BlockSpec(memory_space=pltpu.VMEM),
        compiler_params=pltpu.CompilerParams(vmem_limit_bytes=4 * MIB),
        name="merge",
    )(came)

def finish_kernel(in_ref, o_ref, turned_ref):
    out, _, total = merged(in_ref)
    turned_ref[...] = (out / total).T
    tokens = o_ref.shape[1]
    heads = [turned_ref[pl.ds(h, tokens, stride=GROUP), :] for h in range(GROUP)]
    rows = jnp.concatenate(heads, axis=1).astype(bf16)
    for i in range(o_ref.shape[0]):
        o_ref[i] = rows

def finish(came, copies):
    return pl.pallas_call(
        finish_kernel,
        out_shape=jax.ShapeDtypeStruct((copies, HD // GROUP, GROUP * HD), bf16),
        in_specs=in_vmem(1),
        out_specs=pl.BlockSpec(memory_space=pltpu.VMEM),
        scratch_shapes=[pltpu.VMEM((HD, HD), f32)],
        compiler_params=pltpu.CompilerParams(vmem_limit_bytes=4 * MIB),
        name="finish",
    )(came)

def project_kernel(a_ref, w_ref, o_ref):
    owners, tokens, depth = a_ref.shape
    rows = a_ref[...].astype(f32).reshape(owners * tokens, depth).astype(bf16)
    out = jnp.dot(rows, w_ref[...], preferred_element_type=f32)
    for x in range(4):
        for zh in range(ZH):
            for zl in range(ZL):
                at = ((x * ZL + zl) * ZH + zh) * 2
                to = (zh % 2) * 8 + zl * 2
                o_ref[x * 2 + zh // 2, to : to + 2, :] = out[at : at + 2]

def project(rows, weight):
    return pl.pallas_call(
        project_kernel,
        out_shape=jax.ShapeDtypeStruct((8, 16, weight.shape[1]), f32),
        in_specs=in_vmem(2),
        out_specs=pl.BlockSpec(memory_space=pltpu.VMEM),
        compiler_params=pltpu.CompilerParams(vmem_limit_bytes=8 * MIB),
        name="project",
    )(rows, weight)


def exchange(parts, axes, groups=None):
    return lax.all_to_all(
        parts, axes, split_axis=0, concat_axis=0, axis_index_groups=groups, tiled=True
    )


def spread(part, axes, count):
    return exchange(jnp.broadcast_to(part[None], (count,) + part.shape), axes)


def per_device(queries, cache_keys, cache_values, out_weight, cached_length, start):
    count = cache_keys.shape[0]
    x, c = lax.axis_index("x"), lax.axis_index("c")
    z = lax.axis_index(("zh", "zl"))
    depth = ZH * ZL
    pair, far_x = jnp.where(c == 0, x ^ 1, 3 - x), jnp.where(c == 0, 3 - x, x ^ 1)
    rank = jnp.where(c == 0, x & 1, x >> 1)
    near_base, far_base = (x * depth + z) * count, (far_x * depth + z) * count
    info = jnp.stack([x, pair, rank, near_base, far_base, cached_length[0], start[0]])
    info = info.astype(jnp.int32)
    far_keys = lax.ppermute(cache_keys, ("c", "x"), SWAP)
    far_values = lax.ppermute(cache_values, ("c", "x"), SWAP)
    own = spread(queries.reshape(2 * GROUP, HD), ("zh", "zl"), depth)
    own = own.reshape(depth * 2 * GROUP, HD)
    other = lax.ppermute(own, ("c", "x"), SHARE)
    parts = attend(info, own, other, cache_keys, cache_values, far_keys, far_values)
    came = exchange(parts, ("c", "x", "zl"), OWNER_GROUPS)
    came = exchange(merge(came, ZH), ("zh",))
    attention = exchange(finish(came, OWNERS), ("x", "zl"))
    partial_out = exchange(project(attention, out_weight), ("y", "c"))
    return jnp.sum(partial_out, axis=0).astype(bf16)


def solution(mesh):
    fine = Mesh(mesh.devices.reshape(4, 2, X, ZH, ZL), ("y", "c", "x", "zh", "zl"))
    ctx, kv = ("x", "zh", "zl"), ("y", "c")
    return jax.shard_map(
        per_device,
        mesh=fine,
        in_specs=(P(ctx, kv), P(ctx, kv), P(ctx, kv), P(kv, ctx), P(), P()),
        out_specs=P(kv, ctx),
        check_vma=False,
    )
```

```python
import functools
import math

import jax
import jax.numpy as jnp
from jax import lax
from jax.experimental import pallas as pl
from jax.experimental.pallas import tpu as pltpu
from jax.sharding import Mesh
from jax.sharding import PartitionSpec as P

HD = 128
GROUP = 16
SCALE2 = math.log2(math.e) / math.sqrt(HD)
X, ZH, ZL = 4, 4, 4
OWNERS = X * ZL
STAT = 16
ROWS = HD + STAT
KEY_BLOCK = 256
HIDDEN = -1e30
LOWEST = -1e5
MIB = 2**20
SHARE = [(x, x ^ 1) for x in range(X)] + [(X + x, X + 3 - x) for x in range(X)]
SWAP = [(x, 3 - x) for x in range(X)] + [(X + x, X + (x ^ 1)) for x in range(X)]
OWNER_GROUPS = [
    [(c * X + x) * ZL + zl for x in xs for zl in range(ZL)]
    for c, xs in ((0, (0, 1)), (0, (2, 3)), (1, (0, 3)), (1, (1, 2)))
]

bf16 = jnp.bfloat16
f32 = jnp.float32
ROW_ROW = (((1,), (1,)), ((), ()))
ROW_COL = (((1,), (0,)), ((), ()))

def in_vmem(count):
    return [pl.BlockSpec(memory_space=pltpu.VMEM)] * count

def pack(out, top, total):
    high = total.astype(bf16).astype(f32)
    blank = jnp.zeros((STAT - 3, out.shape[1]), f32)
    return jnp.concatenate([out, top, high, total - high, blank], axis=0).astype(bf16)

def attend_kernel(info_ref, q_ref, k_ref, v_ref, far_ref, *refs, own):
    if own:
        o_ref, vt_ref, hide_ref, s_ref = refs
    else:
        vt_ref, hide_ref, _, o_ref, s_ref = refs
    near = k_ref.shape[0]
    blocks = near // KEY_BLOCK
    x, pair, rank, near_base, far_base, cached_end, span_start = [info_ref[i] for i in range(7)]
    owner, to_rank = (x, rank) if own else (pair, 1 - rank)
    chunks = [(zl0, half) for zl0 in range(0, ZL, 2) for half in range(2)]

    def query_rows(zl0):
        parts = []
        for zl in (zl0, zl0 + 1):
            for zh in range(ZH):
                at = (zh * ZL + zl) * 2 * GROUP
                parts.append(q_ref[at : at + 2 * GROUP, :])
        return jnp.concatenate(parts, axis=0)

    def key_rows(half, span):
        return k_ref[span, :] if half == 0 else far_ref[span, :HD]

    def hide():
        for half, base in ((0, near_base), (1, far_base)):
            pos = base + lax.broadcasted_iota(jnp.int32, (near, HD), 0)
            token = lax.broadcasted_iota(jnp.int32, (near, HD), 1)
            visible = (pos < cached_end) | (pos >= span_start) & (pos <= span_start + token)
            hidden = jnp.where(visible, 0.0, HIDDEN)
            hide_ref[half * near : (half + 1) * near, :] = hidden.astype(bf16)

    def token_rows(zl0):
        row = lax.broadcasted_iota(jnp.int32, (2 * HD, HD), 0)
        col = lax.broadcasted_iota(jnp.int32, (2 * HD, HD), 1)
        zh, zl, t = (row >> 5) & 3, zl0 + (row >> 7), (row >> 4) & 1
        return jnp.where(owner * 32 + zh * 8 + zl * 2 + t == col, 1.0, 0.0).astype(bf16)

    def score(i, masked):
        zl0, half = chunks[i]
        rows = query_rows(zl0)
        if masked:
            rows = jnp.concatenate([rows, token_rows(zl0)], axis=1)
        top = None
        for block in range(blocks):
            at = block * KEY_BLOCK
            left = key_rows(half, slice(at, at + KEY_BLOCK))
            if masked:
                at += half * near
                left = jnp.concatenate([left, hide_ref[at : at + KEY_BLOCK, :]], axis=1)
            s = lax.dot_general(left, rows, ROW_ROW, preferred_element_type=f32)
            s_ref[i % 2, block * KEY_BLOCK : (block + 1) * KEY_BLOCK, :] = s
            here = jnp.max(s.reshape(KEY_BLOCK // 8, 8, s.shape[1]), axis=0)
            top = here if top is None else jnp.maximum(top, here)
        top = jnp.max(top, axis=0, keepdims=True) * SCALE2
        return jnp.maximum(top, LOWEST).astype(bf16).astype(f32)

    def weigh(i, top):
        half = chunks[i][1]
        total = None
        for block in range(blocks):
            at = block * KEY_BLOCK
            w = jnp.exp2(s_ref[i % 2, at : at + KEY_BLOCK, :] * SCALE2 - top).astype(bf16)
            at += half * near
            part = lax.dot_general(
                vt_ref[:, at : at + KEY_BLOCK], w, ROW_COL, preferred_element_type=f32
            )
            total = part if total is None else total + part
        return total

    def send(zl0, first, first_top, second, second_top):
        top = jnp.maximum(first_top, second_top)
        out = first * jnp.exp2(first_top - top) + second * jnp.exp2(second_top - top)
        message = pack(out[:HD], top, out[HD : HD + 1])
        to = to_rank * ZL + zl0
        o_ref[to] = message[:, :HD]
        o_ref[to + 1] = message[:, HD:]

    def run(masked):
        if own and masked:
            hide()
        tops, outs = [score(0, masked)], []
        if own:
            vt_ref[:HD, :near] = v_ref[...].astype(f32).T.astype(bf16)
            vt_ref[:HD, near:] = far_ref[:, HD:].astype(f32).T.astype(bf16)
            vt_ref[HD:, :] = jnp.ones((STAT, 2 * near), bf16)
        for i in range(len(chunks)):
            if i + 1 < len(chunks):
                tops.append(score(i + 1, masked))
            outs.append(weigh(i, tops[i]))
            if i % 2:
                send(chunks[i][0], outs[i - 1], tops[i - 1], outs[i], tops[i])

    whole = (near_base + near <= cached_end) & (far_base + near <= cached_end)
    pl.when(whole)(lambda: run(False))
    pl.when(jnp.logical_not(whole))(lambda: run(True))


def attend(info, queries, keys, values, far, earlier=None):
    own = earlier is None
    count = 2 * keys.shape[0]
    message = jax.ShapeDtypeStruct((2 * ZL, ROWS, HD), bf16)
    turned = jax.ShapeDtypeStruct((ROWS, count), bf16)
    hidden = jax.ShapeDtypeStruct((count, HD), bf16)
    operands = [info, queries, keys, values, far]
    if not own:
        parts, turned_values, mask = earlier
        operands += [turned_values, mask, parts]
    return pl.pallas_call(
        functools.partial(attend_kernel, own=own),
        out_shape=(message, turned, hidden) if own else message,
        in_specs=[pl.BlockSpec(memory_space=pltpu.SMEM)] + in_vmem(len(operands) - 1),
        out_specs=tuple(in_vmem(3)) if own else in_vmem(1)[0],
        scratch_shapes=[pltpu.VMEM((2, count // 2, 2 * HD), f32)],
        input_output_aliases={} if own else {7: 0},
        compiler_params=pltpu.CompilerParams(vmem_limit_bytes=14 * MIB),
        cost_estimate=pl.CostEstimate(
            flops=4 * queries.shape[0] * count * HD,
            bytes_accessed=4 * MIB,
            transcendentals=queries.shape[0] * count,
        ),
        name="attend_own" if own else "attend_other",
    )(*operands)


def merged(in_ref):
    senders = in_ref.shape[0]
    stats = [in_ref[i, HD:, :].astype(f32) for i in range(senders)]
    tops = [s[0:1] for s in stats]
    top = tops[0]
    for other in tops[1:]:
        top = jnp.maximum(top, other)
    out, total = None, None
    for i in range(senders):
        keep = jnp.exp2(tops[i] - top)
        part = in_ref[i, :HD, :].astype(f32) * keep
        part_sum = (stats[i][1:2] + stats[i][2:3]) * keep
        out = part if out is None else out + part
        total = part_sum if total is None else total + part_sum
    return out, top, total

def merge_kernel(in_ref, o_ref):
    message = pack(*merged(in_ref))
    for i in range(o_ref.shape[0]):
        o_ref[i] = message

def merge(came, copies):
    return pl.pallas_call(
        merge_kernel,
        out_shape=jax.ShapeDtypeStruct((copies, ROWS, HD), bf16),
        in_specs=in_vmem(1),
        out_specs=pl.BlockSpec(memory_space=pltpu.VMEM),
        compiler_params=pltpu.CompilerParams(vmem_limit_bytes=4 * MIB),
        name="merge",
    )(came)

def finish_kernel(in_ref, o_ref, turned_ref):
    out, _, total = merged(in_ref)
    turned_ref[...] = (out / total).T
    tokens = o_ref.shape[1]
    heads = [turned_ref[pl.ds(h, tokens, stride=GROUP), :] for h in range(GROUP)]
    rows = jnp.concatenate(heads, axis=1).astype(bf16)
    for i in range(o_ref.shape[0]):
        o_ref[i] = rows

def finish(came, copies):
    return pl.pallas_call(
        finish_kernel,
        out_shape=jax.ShapeDtypeStruct((copies, HD // GROUP, GROUP * HD), bf16),
        in_specs=in_vmem(1),
        out_specs=pl.BlockSpec(memory_space=pltpu.VMEM),
        scratch_shapes=[pltpu.VMEM((HD, HD), f32)],
        compiler_params=pltpu.CompilerParams(vmem_limit_bytes=4 * MIB),
        name="finish",
    )(came)

def project_kernel(a_ref, w_ref, o_ref):
    owners, tokens, depth = a_ref.shape
    rows = a_ref[...].astype(f32).reshape(owners * tokens, depth).astype(bf16)
    out = jnp.dot(rows, w_ref[...], preferred_element_type=f32)
    for x in range(4):
        for zh in range(ZH):
            for zl in range(ZL):
                at = ((x * ZL + zl) * ZH + zh) * 2
                to = (zh % 2) * 8 + zl * 2
                o_ref[x * 2 + zh // 2, to : to + 2, :] = out[at : at + 2]

def project(rows, weight):
    return pl.pallas_call(
        project_kernel,
        out_shape=jax.ShapeDtypeStruct((8, 16, weight.shape[1]), f32),
        in_specs=in_vmem(2),
        out_specs=pl.BlockSpec(memory_space=pltpu.VMEM),
        compiler_params=pltpu.CompilerParams(vmem_limit_bytes=8 * MIB),
        name="project",
    )(rows, weight)


def exchange(parts, axes, groups=None):
    return lax.all_to_all(
        parts, axes, split_axis=0, concat_axis=0, axis_index_groups=groups, tiled=True
    )


def spread(part, axes, count):
    return exchange(jnp.broadcast_to(part[None], (count,) + part.shape), axes)


def per_device(queries, cache_keys, cache_values, out_weight, cached_length, start):
    count = cache_keys.shape[0]
    x, c = lax.axis_index("x"), lax.axis_index("c")
    z = lax.axis_index(("zh", "zl"))
    depth = ZH * ZL
    pair, far_x = jnp.where(c == 0, x ^ 1, 3 - x), jnp.where(c == 0, 3 - x, x ^ 1)
    rank = jnp.where(c == 0, x & 1, x >> 1)
    near_base, far_base = (x * depth + z) * count, (far_x * depth + z) * count
    info = jnp.stack([x, pair, rank, near_base, far_base, cached_length[0], start[0]])
    info = info.astype(jnp.int32)
    cache = jnp.concatenate([cache_keys, cache_values], axis=1)
    cache, queries = lax.optimization_barrier((cache, queries))
    far = lax.ppermute(cache, ("c", "x"), SWAP)
    own = spread(queries.reshape(2 * GROUP, HD), ("zh", "zl"), depth)
    own = own.reshape(depth * 2 * GROUP, HD)
    other = lax.ppermute(own, ("c", "x"), SHARE)
    earlier = attend(info, own, cache_keys, cache_values, far)
    parts = attend(info, other, cache_keys, cache_values, far, earlier)
    came = exchange(parts, ("c", "x", "zl"), OWNER_GROUPS)
    came = exchange(merge(came, ZH), ("zh",))
    attention = exchange(finish(came, OWNERS), ("x", "zl"))
    partial_out = exchange(project(attention, out_weight), ("y", "c"))
    return jnp.sum(partial_out, axis=0).astype(bf16)


def solution(mesh):
    fine = Mesh(mesh.devices.reshape(4, 2, X, ZH, ZL), ("y", "c", "x", "zh", "zl"))
    ctx, kv = ("x", "zh", "zl"), ("y", "c")
    return jax.shard_map(
        per_device,
        mesh=fine,
        in_specs=(P(ctx, kv), P(ctx, kv), P(ctx, kv), P(kv, ctx), P(), P()),
        out_specs=P(kv, ctx),
        check_vma=False,
    )
```

```python
import math

import jax
import jax.numpy as jnp
from jax import lax
from jax.experimental import pallas as pl
from jax.experimental.pallas import tpu as pltpu
from jax.sharding import Mesh
from jax.sharding import PartitionSpec as P

HD = 128
GROUP = 16
SCALE2 = math.log2(math.e) / math.sqrt(HD)
XA, XB, ZH, ZL = 2, 2, 4, 4
STAT = 16
ROWS = HD + STAT
KEY_BLOCK = 256
HIDDEN = -1e30
LOWEST = -1e5
MIB = 2**20

bf16 = jnp.bfloat16
f32 = jnp.float32
ROW_ROW = (((1,), (1,)), ((), ()))
ROW_COL = (((1,), (0,)), ((), ()))

def in_vmem(count):
    return [pl.BlockSpec(memory_space=pltpu.VMEM)] * count

def pack(out, top, total):
    high = total.astype(bf16).astype(f32)
    blank = jnp.zeros((STAT - 3, out.shape[1]), f32)
    return jnp.concatenate([out, top, high, total - high, blank], axis=0).astype(bf16)

def ctx_x():
    return lax.axis_index("xa") * XB + lax.axis_index("xb")


def attend_kernel(
    cached_ref, start_ref, qa_ref, qb_ref, near_ref, far_ref, o_ref, vt_ref, s_ref, hide_ref
):
    near = near_ref.shape[0]
    keys = 2 * near
    blocks = near // KEY_BLOCK
    x, z = ctx_x(), lax.axis_index("zh") * ZL + lax.axis_index("zl")
    near_base, far_base = (x * ZH * ZL + z) * near, ((3 - x) * ZH * ZL + z) * near
    cached_end, span_start = cached_ref[0], start_ref[0]
    vt_ref[:HD, :near] = near_ref[:, HD:].astype(f32).T.astype(bf16)
    vt_ref[:HD, near:] = far_ref[:, HD:].astype(f32).T.astype(bf16)
    vt_ref[HD:, :] = jnp.ones((STAT, keys), bf16)

    def query_rows(zl):
        parts = []
        for t in range(2):
            for ref in (qa_ref, qb_ref):
                for zh in range(ZH):
                    at = ((zh * ZL + zl) * 2 + t) * GROUP
                    parts.append(ref[at : at + GROUP, :])
        return jnp.concatenate(parts, axis=0)

    def key_rows(block):
        at = block * KEY_BLOCK
        if at < near:
            return near_ref[at : at + KEY_BLOCK, :HD]
        return far_ref[at - near : at - near + KEY_BLOCK, :HD]

    def hide():
        for half, base in ((0, near_base), (1, far_base)):
            pos = base + lax.broadcasted_iota(jnp.int32, (near, HD), 0)
            token = lax.broadcasted_iota(jnp.int32, (near, HD), 1)
            visible = (pos < cached_end) | (pos >= span_start) & (pos <= span_start + token)
            hide_ref[half * near : (half + 1) * near, :] = jnp.where(visible, 0.0, HIDDEN).astype(bf16)

    def token_rows(zl):
        row = lax.broadcasted_iota(jnp.int32, (2 * HD, HD), 0)
        col = lax.broadcasted_iota(jnp.int32, (2 * HD, HD), 1)
        t, owner, zh = row >> 7, x ^ ((row >> 6) & 1), (row >> 4) & 3
        return jnp.where(owner * 32 + zh * 8 + zl * 2 + t == col, 1.0, 0.0).astype(bf16)

    def score(i, masked):
        zl, half = divmod(i, 2)
        rows = query_rows(zl)
        if masked:
            rows = jnp.concatenate([rows, token_rows(zl)], axis=1)
        top = None
        for block in range(blocks):
            at = half * near + block * KEY_BLOCK
            left = key_rows(at // KEY_BLOCK)
            if masked:
                left = jnp.concatenate([left, hide_ref[at : at + KEY_BLOCK, :]], axis=1)
            s = lax.dot_general(left, rows, ROW_ROW, preferred_element_type=f32)
            s_ref[i % 2, block * KEY_BLOCK : (block + 1) * KEY_BLOCK, :] = s
            here = jnp.max(s.reshape(KEY_BLOCK // 8, 8, s.shape[1]), axis=0)
            top = here if top is None else jnp.maximum(top, here)
        top = jnp.max(top, axis=0, keepdims=True) * SCALE2
        return jnp.maximum(top, LOWEST).astype(bf16).astype(f32)

    def weigh(i, top):
        total = None
        for block in range(blocks):
            at = block * KEY_BLOCK
            w = jnp.exp2(s_ref[i % 2, at : at + KEY_BLOCK, :] * SCALE2 - top).astype(bf16)
            at += i % 2 * near
            part = lax.dot_general(
                vt_ref[:, at : at + KEY_BLOCK], w, ROW_COL, preferred_element_type=f32
            )
            total = part if total is None else total + part
        return total

    def send(zl, first, first_top, second, second_top):
        top = jnp.maximum(first_top, second_top)
        out = first * jnp.exp2(first_top - top) + second * jnp.exp2(second_top - top)
        message = pack(out[:HD], top, out[HD : HD + 1])
        o_ref[zl] = message[:, :HD]
        o_ref[ZL + zl] = message[:, HD:]

    def run(masked):
        if masked:
            hide()
        tops, outs = [score(0, masked)], []
        for i in range(2 * ZL):
            if i + 1 < 2 * ZL:
                tops.append(score(i + 1, masked))
            outs.append(weigh(i, tops[i]))
            if i % 2:
                send(i // 2, outs[i - 1], tops[i - 1], outs[i], tops[i])

    whole = (near_base + near <= cached_end) & (far_base + near <= cached_end)
    pl.when(whole)(lambda: run(False))
    pl.when(jnp.logical_not(whole))(lambda: run(True))

def attend(cached_length, start, qa, qb, near, far):
    count = 2 * near.shape[0]
    return pl.pallas_call(
        attend_kernel,
        out_shape=jax.ShapeDtypeStruct((XB * ZL, ROWS, HD), bf16),
        in_specs=[pl.BlockSpec(memory_space=pltpu.SMEM)] * 2 + in_vmem(4),
        out_specs=pl.BlockSpec(memory_space=pltpu.VMEM),
        scratch_shapes=[
            pltpu.VMEM((ROWS, count), bf16),
            pltpu.VMEM((2, count // 2, 2 * HD), f32),
            pltpu.VMEM((count, HD), bf16),
        ],
        compiler_params=pltpu.CompilerParams(vmem_limit_bytes=14 * MIB),
        name="attend",
    )(cached_length, start, qa, qb, near, far)

def merged(messages):
    tops = [m[HD : HD + 1] for m in messages]
    top = tops[0]
    for other in tops[1:]:
        top = jnp.maximum(top, other)
    out, total = None, None
    for m, own in zip(messages, tops):
        keep = jnp.exp2(own - top)
        part, part_sum = m[:HD] * keep, (m[HD + 1 : HD + 2] + m[HD + 2 : HD + 3]) * keep
        out = part if out is None else out + part
        total = part_sum if total is None else total + part_sum
    return out, top, total


def merge_kernel(in_ref, o_ref):
    messages = [in_ref[i].astype(f32) for i in range(XB * ZL)]
    half = HD // 2
    for i in range(ZL, XB * ZL):
        messages[i] = jnp.concatenate([messages[i][:, half:], messages[i][:, :half]], axis=1)
    message = pack(*merged(messages))
    for i in range(o_ref.shape[0]):
        o_ref[i] = message

def merge(came, copies):
    return pl.pallas_call(
        merge_kernel,
        out_shape=jax.ShapeDtypeStruct((copies, ROWS, HD), bf16),
        in_specs=in_vmem(1),
        out_specs=pl.BlockSpec(memory_space=pltpu.VMEM),
        compiler_params=pltpu.CompilerParams(vmem_limit_bytes=4 * MIB),
        name="merge",
    )(came)

def finish_kernel(in_ref, o_ref, turned_ref):
    out, _, total = merged([in_ref[i].astype(f32) for i in range(in_ref.shape[0])])
    turned_ref[...] = (out / total).T
    tokens = o_ref.shape[1]
    heads = [turned_ref[pl.ds(h, tokens, stride=GROUP), :] for h in range(GROUP)]
    rows = jnp.concatenate(heads, axis=1).astype(bf16)
    for i in range(o_ref.shape[0]):
        o_ref[i] = rows

def finish(came, copies):
    return pl.pallas_call(
        finish_kernel,
        out_shape=jax.ShapeDtypeStruct((copies, HD // GROUP, GROUP * HD), bf16),
        in_specs=in_vmem(1),
        out_specs=pl.BlockSpec(memory_space=pltpu.VMEM),
        scratch_shapes=[pltpu.VMEM((HD, HD), f32)],
        compiler_params=pltpu.CompilerParams(vmem_limit_bytes=4 * MIB),
        name="finish",
    )(came)

def project_kernel(a_ref, own_ref, other_ref, o_ref):
    senders, tokens, depth = a_ref.shape
    xb = lax.axis_index("xb")
    rows = a_ref[...].astype(f32).reshape(senders * tokens, depth).astype(bf16)
    for to, w_ref in ((xb, own_ref), (1 - xb, other_ref)):
        out = jnp.dot(rows, w_ref[...], preferred_element_type=f32)
        for x in range(XA * XB):
            for half in range(2):
                parts = []
                for zl in range(ZL):
                    at = (x // XB * ZL + zl) * tokens + x % XB * ZH + half * 2
                    parts.append(out[at : at + 2])
                o_ref[(x * 2 + half) * XB + to] = jnp.concatenate(parts, axis=0)


def project(rows, weight, other):
    return pl.pallas_call(
        project_kernel,
        out_shape=jax.ShapeDtypeStruct((8 * XB, 8, weight.shape[1]), f32),
        in_specs=in_vmem(3),
        out_specs=pl.BlockSpec(memory_space=pltpu.VMEM),
        compiler_params=pltpu.CompilerParams(vmem_limit_bytes=8 * MIB),
        name="project",
    )(rows, weight, other)


def total_kernel(in_ref, o_ref, s_ref):
    for t in range(2):
        out = in_ref[t]
        for sender in range(XB + t, in_ref.shape[0], XB):
            out = out + in_ref[sender]
        for zl in range(ZL):
            for zh in range(2):
                to = (zh * ZL + zl) * 2 + t
                s_ref[to : to + 1, :] = out[zl * 2 + zh : zl * 2 + zh + 1]
    o_ref[...] = s_ref[...].astype(bf16)


def total(came):
    columns = came.shape[2]
    return pl.pallas_call(
        total_kernel,
        out_shape=jax.ShapeDtypeStruct((16, columns), bf16),
        in_specs=in_vmem(1),
        out_specs=pl.BlockSpec(memory_space=pltpu.VMEM),
        scratch_shapes=[pltpu.VMEM((16, columns), f32)],
        compiler_params=pltpu.CompilerParams(vmem_limit_bytes=2 * MIB),
        name="total",
    )(came)


def exchange(parts, axes):
    return lax.all_to_all(parts, axes, split_axis=0, concat_axis=0, tiled=True)


def per_device(queries, cache_keys, cache_values, out_weight, cached_length, start):
    swap = [(0, 1), (1, 0)]
    near = jnp.concatenate([cache_keys, cache_values], axis=1)
    near, queries = lax.optimization_barrier((near, queries))
    rows = jnp.broadcast_to(queries.reshape(1, 2 * GROUP, HD), (ZH * ZL, 2 * GROUP, HD))
    far = lax.ppermute(near, ("xa", "xb"), [(0, 3), (3, 0), (1, 2), (2, 1)])
    own = exchange(rows, ("zh", "zl")).reshape(ZH * ZL * 2 * GROUP, HD)
    other = lax.ppermute(own, "xb", swap)
    other_weight = lax.ppermute(out_weight, "xb", swap)
    came = exchange(attend(cached_length, start, own, other, near, far), ("xb", "zl"))
    came = exchange(merge(came, ZH), ("zh",))
    done, other_weight = lax.optimization_barrier((finish(came, XA * ZL), other_weight))
    attention = exchange(done, ("xa", "zl"))
    return total(exchange(project(attention, out_weight, other_weight), ("y", "c", "xb")))


def solution(mesh):
    shape = (4, 2, XA, XB, ZH, ZL)
    fine = Mesh(mesh.devices.reshape(shape), ("y", "c", "xa", "xb", "zh", "zl"))
    ctx, kv = ("xa", "xb", "zh", "zl"), ("y", "c")
    return jax.shard_map(
        per_device,
        mesh=fine,
        in_specs=(P(ctx, kv), P(ctx, kv), P(ctx, kv), P(kv, ctx), P(), P()),
        out_specs=P(kv, ctx),
        check_vma=False,
    )
```

```python
import math

import jax
import jax.numpy as jnp
from jax import lax
from jax.experimental import pallas as pl
from jax.experimental.pallas import tpu as pltpu
from jax.sharding import Mesh
from jax.sharding import PartitionSpec as P

HD = 128
GROUP = 16
SCALE2 = math.log2(math.e) / math.sqrt(HD)
XA, XB, ZH, ZL = 2, 2, 4, 4
STAT = 8
ONES = 16
ROWS = HD + STAT
KEY_BLOCK = 256
HIDDEN = -1e30
LOWEST = -1e5
MIB = 2**20

bf16 = jnp.bfloat16
f32 = jnp.float32
ROW_ROW = (((1,), (1,)), ((), ()))
ROW_COL = (((1,), (0,)), ((), ()))

def in_vmem(count):
    return [pl.BlockSpec(memory_space=pltpu.VMEM)] * count

def pack(out, top, total):
    high = total.astype(bf16).astype(f32)
    blank = jnp.zeros((STAT - 3, out.shape[1]), f32)
    return jnp.concatenate([out, top, high, total - high, blank], axis=0).astype(bf16)

def ctx_x():
    return lax.axis_index("xa") * XB + lax.axis_index("xb")


def attend_kernel(
    cached_ref, start_ref, qa_ref, qb_ref, near_ref, far_ref, o_ref, vt_ref, s_ref, hide_ref
):
    near = near_ref.shape[0]
    keys = 2 * near
    blocks = near // KEY_BLOCK
    x, z = ctx_x(), lax.axis_index("zh") * ZL + lax.axis_index("zl")
    near_base, far_base = (x * ZH * ZL + z) * near, ((3 - x) * ZH * ZL + z) * near
    cached_end, span_start = cached_ref[0], start_ref[0]

    def query_rows(zl):
        parts = []
        for t in range(2):
            for ref in (qa_ref, qb_ref):
                for zh in range(ZH):
                    at = ((zh * ZL + zl) * 2 + t) * GROUP
                    parts.append(ref[at : at + GROUP, :])
        return jnp.concatenate(parts, axis=0)

    def key_rows(block):
        at = block * KEY_BLOCK
        if at < near:
            return near_ref[at : at + KEY_BLOCK, :HD]
        return far_ref[at - near : at - near + KEY_BLOCK, :HD]

    def hide():
        for half, base in ((0, near_base), (1, far_base)):
            pos = base + lax.broadcasted_iota(jnp.int32, (near, HD), 0)
            token = lax.broadcasted_iota(jnp.int32, (near, HD), 1)
            visible = (pos < cached_end) | (pos >= span_start) & (pos <= span_start + token)
            hide_ref[half * near : (half + 1) * near, :] = jnp.where(visible, 0.0, HIDDEN).astype(bf16)

    def token_rows(zl):
        row = lax.broadcasted_iota(jnp.int32, (2 * HD, HD), 0)
        col = lax.broadcasted_iota(jnp.int32, (2 * HD, HD), 1)
        t, owner, zh = row >> 7, x ^ ((row >> 6) & 1), (row >> 4) & 3
        return jnp.where(owner * 32 + zh * 8 + zl * 2 + t == col, 1.0, 0.0).astype(bf16)

    def score(i, masked):
        zl, half = divmod(i, 2)
        rows = query_rows(zl)
        if masked:
            rows = jnp.concatenate([rows, token_rows(zl)], axis=1)
        top = None
        for block in range(blocks):
            at = half * near + block * KEY_BLOCK
            left = key_rows(at // KEY_BLOCK)
            if masked:
                left = jnp.concatenate([left, hide_ref[at : at + KEY_BLOCK, :]], axis=1)
            s = lax.dot_general(left, rows, ROW_ROW, preferred_element_type=f32)
            s_ref[i % 2, block * KEY_BLOCK : (block + 1) * KEY_BLOCK, :] = s
            here = jnp.max(s.reshape(KEY_BLOCK // 8, 8, s.shape[1]), axis=0)
            top = here if top is None else jnp.maximum(top, here)
        top = jnp.max(top, axis=0, keepdims=True) * SCALE2
        return jnp.maximum(top, LOWEST).astype(bf16).astype(f32)

    def weigh(i, top):
        total = None
        for block in range(blocks):
            at = block * KEY_BLOCK
            w = jnp.exp2(s_ref[i % 2, at : at + KEY_BLOCK, :] * SCALE2 - top).astype(bf16)
            at += i % 2 * near
            part = lax.dot_general(
                vt_ref[:, at : at + KEY_BLOCK], w, ROW_COL, preferred_element_type=f32
            )
            total = part if total is None else total + part
        return total

    def send(zl, first, first_top, second, second_top):
        top = jnp.maximum(first_top, second_top)
        out = first * jnp.exp2(first_top - top) + second * jnp.exp2(second_top - top)
        message = pack(out[:HD], top, out[HD : HD + 1])
        o_ref[zl] = message[:, :HD]
        o_ref[ZL + zl] = message[:, HD:]

    def run(masked):
        if masked:
            hide()
        tops, outs = [score(0, masked)], []
        vt_ref[:HD, :near] = near_ref[:, HD:].astype(f32).T.astype(bf16)
        vt_ref[:HD, near:] = far_ref[:, HD:].astype(f32).T.astype(bf16)
        vt_ref[HD:, :] = jnp.ones((ONES, keys), bf16)
        for i in range(2 * ZL):
            if i + 1 < 2 * ZL:
                tops.append(score(i + 1, masked))
            outs.append(weigh(i, tops[i]))
            if i % 2:
                send(i // 2, outs[i - 1], tops[i - 1], outs[i], tops[i])

    whole = (near_base + near <= cached_end) & (far_base + near <= cached_end)
    pl.when(whole)(lambda: run(False))
    pl.when(jnp.logical_not(whole))(lambda: run(True))

def attend(cached_length, start, qa, qb, near, far):
    count = 2 * near.shape[0]
    return pl.pallas_call(
        attend_kernel,
        out_shape=jax.ShapeDtypeStruct((XB * ZL, ROWS, HD), bf16),
        in_specs=[pl.BlockSpec(memory_space=pltpu.SMEM)] * 2 + in_vmem(4),
        out_specs=pl.BlockSpec(memory_space=pltpu.VMEM),
        scratch_shapes=[
            pltpu.VMEM((HD + ONES, count), bf16),
            pltpu.VMEM((2, count // 2, 2 * HD), f32),
            pltpu.VMEM((count, HD), bf16),
        ],
        compiler_params=pltpu.CompilerParams(vmem_limit_bytes=14 * MIB),
        name="attend",
    )(cached_length, start, qa, qb, near, far)

def merged(messages):
    tops = [m[HD : HD + 1] for m in messages]
    top = tops[0]
    for other in tops[1:]:
        top = jnp.maximum(top, other)
    out, total = None, None
    for m, own in zip(messages, tops):
        keep = jnp.exp2(own - top)
        part, part_sum = m[:HD] * keep, (m[HD + 1 : HD + 2] + m[HD + 2 : HD + 3]) * keep
        out = part if out is None else out + part
        total = part_sum if total is None else total + part_sum
    return out, top, total


def merge_kernel(in_ref, o_ref):
    messages = [in_ref[i].astype(f32) for i in range(XB * ZL)]
    half = HD // 2
    for i in range(ZL, XB * ZL):
        messages[i] = jnp.concatenate([messages[i][:, half:], messages[i][:, :half]], axis=1)
    message = pack(*merged(messages))
    for i in range(o_ref.shape[0]):
        o_ref[i] = message

def merge(came, copies):
    return pl.pallas_call(
        merge_kernel,
        out_shape=jax.ShapeDtypeStruct((copies, ROWS, HD), bf16),
        in_specs=in_vmem(1),
        out_specs=pl.BlockSpec(memory_space=pltpu.VMEM),
        compiler_params=pltpu.CompilerParams(vmem_limit_bytes=4 * MIB),
        name="merge",
    )(came)

def finish_kernel(in_ref, o_ref, turned_ref):
    out, _, total = merged([in_ref[i].astype(f32) for i in range(in_ref.shape[0])])
    turned_ref[...] = (out / total).T
    tokens = o_ref.shape[1]
    heads = [turned_ref[pl.ds(h, tokens, stride=GROUP), :] for h in range(GROUP)]
    rows = jnp.concatenate(heads, axis=1).astype(bf16)
    for i in range(o_ref.shape[0]):
        o_ref[i] = rows

def finish(came, copies):
    return pl.pallas_call(
        finish_kernel,
        out_shape=jax.ShapeDtypeStruct((copies, HD // GROUP, GROUP * HD), bf16),
        in_specs=in_vmem(1),
        out_specs=pl.BlockSpec(memory_space=pltpu.VMEM),
        scratch_shapes=[pltpu.VMEM((HD, HD), f32)],
        compiler_params=pltpu.CompilerParams(vmem_limit_bytes=4 * MIB),
        name="finish",
    )(came)

def project_kernel(a_ref, own_ref, other_ref, o_ref):
    senders, tokens, depth = a_ref.shape
    xb = lax.axis_index("xb")
    rows = a_ref[...].astype(f32).reshape(senders * tokens, depth).astype(bf16)
    for to, w_ref in ((xb, own_ref), (1 - xb, other_ref)):
        out = jnp.dot(rows, w_ref[...], preferred_element_type=f32)
        for x in range(XA * XB):
            for half in range(2):
                parts = []
                for zl in range(ZL):
                    at = (x // XB * ZL + zl) * tokens + x % XB * ZH + half * 2
                    parts.append(out[at : at + 2])
                o_ref[(x * 2 + half) * XB + to] = jnp.concatenate(parts, axis=0)


def project(rows, weight, other):
    return pl.pallas_call(
        project_kernel,
        out_shape=jax.ShapeDtypeStruct((8 * XB, 8, weight.shape[1]), f32),
        in_specs=in_vmem(3),
        out_specs=pl.BlockSpec(memory_space=pltpu.VMEM),
        compiler_params=pltpu.CompilerParams(vmem_limit_bytes=8 * MIB),
        name="project",
    )(rows, weight, other)


def total_kernel(in_ref, o_ref, s_ref):
    for t in range(2):
        out = in_ref[t]
        for sender in range(XB + t, in_ref.shape[0], XB):
            out = out + in_ref[sender]
        for zl in range(ZL):
            for zh in range(2):
                to = (zh * ZL + zl) * 2 + t
                s_ref[to : to + 1, :] = out[zl * 2 + zh : zl * 2 + zh + 1]
    o_ref[...] = s_ref[...].astype(bf16)


def total(came):
    columns = came.shape[2]
    return pl.pallas_call(
        total_kernel,
        out_shape=jax.ShapeDtypeStruct((16, columns), bf16),
        in_specs=in_vmem(1),
        out_specs=pl.BlockSpec(memory_space=pltpu.VMEM),
        scratch_shapes=[pltpu.VMEM((16, columns), f32)],
        compiler_params=pltpu.CompilerParams(vmem_limit_bytes=2 * MIB),
        name="total",
    )(came)


def exchange(parts, axes):
    return lax.all_to_all(parts, axes, split_axis=0, concat_axis=0, tiled=True)


def per_device(queries, cache_keys, cache_values, out_weight, cached_length, start):
    swap = [(0, 1), (1, 0)]
    near = jnp.concatenate([cache_keys, cache_values], axis=1)
    near, queries = lax.optimization_barrier((near, queries))
    rows = jnp.broadcast_to(queries.reshape(1, 2 * GROUP, HD), (ZH * ZL, 2 * GROUP, HD))
    far = lax.ppermute(near, ("xa", "xb"), [(0, 3), (3, 0), (1, 2), (2, 1)])
    own = exchange(rows, ("zh", "zl")).reshape(ZH * ZL * 2 * GROUP, HD)
    other = lax.ppermute(own, "xb", swap)
    other_weight = lax.ppermute(out_weight, "xb", swap)
    came = exchange(attend(cached_length, start, own, other, near, far), ("xb", "zl"))
    came = exchange(merge(came, ZH), ("zh",))
    done, other_weight = lax.optimization_barrier((finish(came, XA * ZL), other_weight))
    attention = exchange(done, ("xa", "zl"))
    return total(exchange(project(attention, out_weight, other_weight), ("y", "c", "xb")))


def solution(mesh):
    shape = (4, 2, XA, XB, ZH, ZL)
    fine = Mesh(mesh.devices.reshape(shape), ("y", "c", "xa", "xb", "zh", "zl"))
    ctx, kv = ("xa", "xb", "zh", "zl"), ("y", "c")
    return jax.shard_map(
        per_device,
        mesh=fine,
        in_specs=(P(ctx, kv), P(ctx, kv), P(ctx, kv), P(kv, ctx), P(), P()),
        out_specs=P(kv, ctx),
        check_vma=False,
    )
```
